32 devices in a mesh: mod: 4 (over z), row: 8 (over y, x, core).
Axes of the slice: x: 2, y: 2, z: 4, core: 2. Of those that a mesh axis runs over, the one named last changes fastest.
Arguments:
- activations: bfloat16 [4, 8192, 4096], P('mod', 'row'), may hold values from -6 to 6
- out_grads: bfloat16 [4, 8192, 4096], P('mod', 'row'), may hold values from -0.3125 to 0.3125
- in_projection: bfloat16 [4, 64, 4096], P('mod'), may hold values from -0.09375 to 0.09375
- out_projection: bfloat16 [4, 64, 4096], P('mod'), may hold values from -0.09375 to 0.09375
- inv_curvature: bfloat16 [4, 4096, 4096], P('mod', 'row'), as said below
- store_grads: bfloat16 [4, 6144, 4096], P('mod', 'row'), may hold values from -0.046875 to 0.046875
- lengths: int32 [32], replicated, may hold values from 64 to 128, as said below
- owners: int32 [32], replicated, may hold values from 0 to 7, as said below
Outputs:
- scores: float32 [32, 6144], P('mod', 'row')
The draws below stay inside these ranges and needn't reach their ends.
Inputs may be any that keep to these rules, and one draw needn't show every extreme that they name: `owners`: at most 8 query examples have the same owner, and some owner has exactly 8. `lengths`: the examples of one owner hold at most 1024 tokens together, and some owner holds exactly 1024. `inv_curvature`: each module's matrix is symmetric.
All inputs are finite; a program needn't handle non-finite values.
Results may differ from the reference program's by a relative error of at most 0.0041.
Values may be sent and summed in bfloat16 or wider, within the bound.
No kernel may reach another device: no remote copies, remote signals or barrier semaphores. Data moves between devices by JAX's collectives and lax.ppermute only.
A program may use at most 128 MiB of HBM per device.

```python
import math
import jax
import jax.numpy as jnp
import numpy as np
from jax import lax

D = 4096
RANK = 64
LEN = 128
MODS = 4
QUERIES = 32
TOK_DEV = 1024
TOKENS = 8192
STORE = 6144
K = 4096
N_ROW = 8


def routing_plan(key):
    base = jax.random.fold_in(key, 23)
    key_owner, key_example, key_length = jax.random.split(base, 3)
    mean = QUERIES // N_ROW
    pattern = np.array([2 * mean, mean, mean // 2, mean // 2])
    per_slot = np.tile(pattern, N_ROW // 4)
    slot_of_rank = np.repeat(np.arange(N_ROW), per_slot)
    shuffled_owners = jax.random.permutation(key_owner, N_ROW).astype(jnp.int32)
    shuffled_examples = jax.random.permutation(key_example, QUERIES)
    owner_by_rank = shuffled_owners[jnp.asarray(slot_of_rank, dtype=jnp.int32)]
    owners = jnp.zeros((QUERIES,), jnp.int32).at[shuffled_examples].set(owner_by_rank)
    drawn = jax.random.randint(key_length, (QUERIES,), LEN // 2, LEN + 1).astype(jnp.int32)
    length_by_rank = jnp.where(jnp.asarray(slot_of_rank == 0), LEN, drawn).astype(jnp.int32)
    lengths = jnp.zeros((QUERIES,), jnp.int32).at[shuffled_examples].set(length_by_rank)
    return (owners, lengths)


def draw_owners(key, part):
    return routing_plan(key)[0]


def draw_lengths(key, part):
    return routing_plan(key)[1]


def draw_inv_curvature(key, part):
    key_noise, key_diag = jax.random.split(jax.random.fold_in(key, 11), 2)
    order = RANK * RANK
    noise = jax.random.normal(key_noise, (MODS, order, order), jnp.float32)
    noise = (noise + jnp.swapaxes(noise, 1, 2)) * (0.4 / math.sqrt(2.0 * order))
    diagonal = jnp.exp(jax.random.uniform(key_diag, (MODS, order), jnp.float32, 0.0, math.log(3.0)))
    index = jnp.arange(order, dtype=jnp.int32)
    on_diag = (index[:, None] == index[None, :]).astype(jnp.float32)
    matrix = noise + diagonal[:, :, None] * on_diag[None, :, :]
    return matrix.astype(jnp.bfloat16)


def levels(rng, dims, cuts, smallest, high):
    level = 1.0
    for axis_at, blocks in cuts:
        draws = jax.random.uniform(jax.random.fold_in(jax.random.fold_in(rng, 6), axis_at), (blocks,), jnp.float32, smallest / len(cuts), high / len(cuts))
        level = level * jnp.repeat(jnp.exp(draws), dims[axis_at] // blocks).reshape((-1,) + (1,) * (len(dims) - 1 - axis_at))
    return level


def normal_values(stream_key, extent, deviation, bound, pieces=(), kind=jnp.bfloat16):
    values = deviation * jax.random.normal(stream_key, extent, jnp.float32)
    if pieces:
        values = values * levels(stream_key, extent, pieces, -0.22, 0.18)
    return jnp.clip(values, -bound, bound).astype(kind)


def setup_inputs(seed: int = 0) -> dict:
    splits = jax.random.split(jax.random.key(seed), 9)
    activations = normal_values(splits[0], (MODS, TOKENS, D), 1.0, 6.0, ((0, 4), (1, 8)))
    out_grads = normal_values(splits[1], (MODS, TOKENS, D), 0.05, 0.3125, ((0, 4), (1, 8)))
    in_projection = normal_values(splits[2], (MODS, RANK, D), D ** -0.5, 0.09375, ((0, 4),))
    out_projection = normal_values(splits[3], (MODS, RANK, D), D ** -0.5, 0.09375, ((0, 4),))
    inv_curvature = draw_inv_curvature(jax.random.fold_in(splits[8], 71), 0)
    store_grads = normal_values(splits[5], (MODS, STORE, K), (K * MODS) ** -0.5, 0.046875, ((0, 4), (1, 8)))
    lengths = draw_lengths(jax.random.fold_in(splits[8], 71), 0)
    owners = draw_owners(jax.random.fold_in(splits[8], 71), 0)
    return dict(activations=activations, out_grads=out_grads, in_projection=in_projection, out_projection=out_projection, inv_curvature=inv_curvature, store_grads=store_grads, lengths=lengths, owners=owners)


exact_mode = lax.Precision.HIGHEST


def contract_last(left, right):
    return lax.dot_general(left, right, (((1,), (1,)), ((), ())), preferred_element_type=jnp.float32)


def reference(activations, out_grads, in_projection, out_projection, inv_curvature, store_grads, lengths, owners):
    examples = jnp.arange(QUERIES, dtype=jnp.int32)
    earlier = (owners[:, None] == owners[None, :]) & (examples[None, :] < examples[:, None])
    offsets = jnp.sum(jnp.where(earlier, lengths[None, :], 0), axis=1).astype(jnp.int32)
    positions = jnp.arange(TOKENS, dtype=jnp.int32)
    row_owner = positions // TOK_DEV
    row_local = positions % TOK_DEV
    membership = ((owners[:, None] == row_owner[None, :])
                  & (row_local[None, :] >= offsets[:, None])
                  & (row_local[None, :] < (offsets + lengths)[:, None])).astype(jnp.float32)

    def one_module(module):
        in_feat = contract_last(activations[module], in_projection[module])
        out_feat = contract_last(out_grads[module], out_projection[module])
        weighted = membership[:, None, :] * out_feat.T[None, :, :]
        per_example = jnp.dot(weighted.reshape(QUERIES * RANK, TOKENS), in_feat, precision=exact_mode)
        feature = per_example.reshape(QUERIES, K).astype(jnp.bfloat16)
        preconditioned = jnp.dot(feature, inv_curvature[module], preferred_element_type=jnp.float32).astype(jnp.bfloat16)
        return contract_last(preconditioned, store_grads[module])

    module_scores = lax.map(one_module, jnp.arange(MODS, dtype=jnp.int32))
    return jnp.sum(module_scores, axis=0)
```

```python
import functools

import jax
import jax.numpy as jnp
from jax import lax
from jax.experimental import pallas as pl
from jax.experimental.pallas import tpu as pltpu
from jax.sharding import PartitionSpec as P

MIB = 1024 * 1024


def contract_last(left, right):
    return lax.dot_general(
        left, right, (((1,), (1,)), ((), ())), preferred_element_type=jnp.float32
    )


def largest_tile(extent, most):
    tile = min(extent, most)
    while extent % tile:
        tile -= 1
    return tile


def split_two(values):
    high = values.astype(jnp.bfloat16).astype(jnp.float32)
    return high, values - high


def featurize_kernel(
    lengths_ref,
    owners_ref,
    act_ref,
    grad_ref,
    in_proj_ref,
    out_proj_ref,
    feature_ref,
    placer_ref,
    total,
    starts,
    stops,
    counts,
):
    step = pl.program_id(0)
    tile = act_ref.shape[0]
    rank = in_proj_ref.shape[0]
    capacity = feature_ref.shape[0]
    queries, slots = placer_ref.shape

    @pl.when(step == 0)
    def _():
        me = lax.axis_index("row")
        for slot in range(capacity):
            starts[slot] = 0
            stops[slot] = 0
        for owner in range(slots // capacity):
            counts[owner] = 0
        used = jnp.int32(0)
        lane = lax.broadcasted_iota(jnp.int32, (1, slots), 1)
        for example in range(queries):
            owner = owners_ref[example]
            length = lengths_ref[example]
            rank_here = counts[owner]
            counts[owner] = rank_here + 1
            mine = owner == me

            @pl.when(mine)
            def _():
                starts[rank_here] = used
                stops[rank_here] = used + length

            used = used + jnp.where(mine, length, 0)
            placer_ref[pl.ds(example, 1), :] = (
                lane == owner * capacity + rank_here
            ).astype(jnp.float32)
        total[...] = jnp.zeros_like(total)

    in_feat = contract_last(act_ref[...], in_proj_ref[...])
    out_feat = contract_last(grad_ref[...], out_proj_ref[...]).T
    slot_id = lax.broadcasted_iota(jnp.int32, (capacity, tile), 0)
    position = step * tile + lax.broadcasted_iota(jnp.int32, (capacity, tile), 1)
    start = jnp.zeros((capacity, tile), jnp.int32)
    stop = jnp.zeros((capacity, tile), jnp.int32)
    for slot in range(capacity):
        start = jnp.where(slot_id == slot, starts[slot], start)
        stop = jnp.where(slot_id == slot, stops[slot], stop)
    member = ((position >= start) & (position < stop)).astype(jnp.float32)
    in_high, in_low = (part.astype(jnp.bfloat16) for part in split_two(in_feat))
    out_high, out_low = (
        (part[:, None, :] * member[None, :, :])
        .reshape(rank * capacity, tile)
        .astype(jnp.bfloat16)
        for part in split_two(out_feat)
    )
    total[...] += (
        jnp.dot(out_high, in_high, preferred_element_type=jnp.float32)
        + jnp.dot(out_high, in_low, preferred_element_type=jnp.float32)
        + jnp.dot(out_low, in_high, preferred_element_type=jnp.float32)
    )

    @pl.when(step == pl.num_programs(0) - 1)
    def _():
        per_store = 2
        for first in range(0, rank, per_store):
            rows = [
                total[pl.ds((first + k) * capacity, capacity), :] for k in range(per_store)
            ]
            feature_ref[:, pl.ds(first * rank, per_store * rank)] = jnp.concatenate(
                rows, axis=1
            ).astype(jnp.bfloat16)


def featurize(activations, out_grads, in_projection, out_projection, lengths, owners, capacity, slots):
    tokens, width = activations.shape
    rank = in_projection.shape[0]
    queries = lengths.shape[0]
    tile = largest_tile(tokens, 256)
    whole = lambda step: (0, 0)
    return pl.pallas_call(
        featurize_kernel,
        grid=(tokens // tile,),
        in_specs=[
            pl.BlockSpec(memory_space=pltpu.SMEM),
            pl.BlockSpec(memory_space=pltpu.SMEM),
            pl.BlockSpec((tile, width), lambda step: (step, 0)),
            pl.BlockSpec((tile, width), lambda step: (step, 0)),
            pl.BlockSpec((rank, width), whole),
            pl.BlockSpec((rank, width), whole),
        ],
        out_specs=[
            pl.BlockSpec((capacity, rank * rank), whole),
            pl.BlockSpec((queries, slots), whole),
        ],
        out_shape=[
            jax.ShapeDtypeStruct((capacity, rank * rank), jnp.bfloat16),
            jax.ShapeDtypeStruct((queries, slots), jnp.float32),
        ],
        scratch_shapes=[
            pltpu.VMEM((rank * capacity, rank), jnp.float32),
            pltpu.SMEM((capacity,), jnp.int32),
            pltpu.SMEM((capacity,), jnp.int32),
            pltpu.SMEM((slots // capacity,), jnp.int32),
        ],
        compiler_params=pltpu.CompilerParams(vmem_limit_bytes=32 * MIB),
        name="featurize",
    )(lengths, owners, activations, out_grads, in_projection, out_projection)


def precondition_kernel(feature_ref, curvature_ref, placer_ref, out_ref, total):
    step = pl.program_id(0)

    @pl.when(step == 0)
    def _():
        total[...] = jnp.zeros_like(total)

    total[...] += contract_last(feature_ref[...], curvature_ref[...])

    @pl.when(step == pl.num_programs(0) - 1)
    def _():
        out_ref[...] = jnp.dot(
            placer_ref[...].astype(jnp.bfloat16),
            total[...].astype(jnp.bfloat16),
            preferred_element_type=jnp.float32,
        ).astype(jnp.bfloat16)


def precondition(gathered, curvature_rows, placer):
    slots, entries = gathered.shape
    columns = curvature_rows.shape[0]
    queries = placer.shape[0]
    depth = largest_tile(entries, 1024)
    return pl.pallas_call(
        precondition_kernel,
        grid=(entries // depth,),
        in_specs=[
            pl.BlockSpec((slots, depth), lambda step: (0, step)),
            pl.BlockSpec((columns, depth), lambda step: (0, step)),
            pl.BlockSpec((queries, slots), lambda step: (0, 0)),
        ],
        out_specs=pl.BlockSpec((queries, columns), lambda step: (0, 0)),
        out_shape=jax.ShapeDtypeStruct((queries, columns), jnp.bfloat16),
        scratch_shapes=[pltpu.VMEM((slots, columns), jnp.float32)],
        compiler_params=pltpu.CompilerParams(vmem_limit_bytes=32 * MIB),
        name="precondition",
    )(gathered, curvature_rows, placer)


def score_kernel(parts, part_ref, store_ref, keep_ref, send_ref, total):
    step = pl.program_id(0)
    share = keep_ref.shape[1]

    @pl.when(step == 0)
    def _():
        total[...] = jnp.zeros_like(total)

    total[...] += contract_last(part_ref[...], store_ref[...])

    @pl.when(step == pl.num_programs(0) - 1)
    def _():
        me = lax.axis_index("mod")
        for place in range(parts):
            row = pl.multiple_of((me ^ place) * share, share)
            block = total[pl.ds(row, share), :]
            if place % 2:
                send_ref[place // 2] = block
            else:
                keep_ref[place // 2] = block


def score(preconditioned, store_rows, queries, parts):
    stores, entries = store_rows.shape
    depth = preconditioned.shape[1]
    share = queries // parts
    half = jax.ShapeDtypeStruct((parts // 2, share, stores), jnp.float32)
    half_spec = pl.BlockSpec((parts // 2, share, stores), lambda step: (0, 0, 0))
    return pl.pallas_call(
        functools.partial(score_kernel, parts),
        grid=(entries // depth,),
        in_specs=[
            pl.BlockSpec((queries, depth), lambda step: (step, 0)),
            pl.BlockSpec((stores, depth), lambda step: (0, step)),
        ],
        out_specs=[half_spec, half_spec],
        out_shape=[half, half],
        scratch_shapes=[pltpu.VMEM((queries, stores), jnp.float32)],
        compiler_params=pltpu.CompilerParams(vmem_limit_bytes=32 * MIB),
        name="score",
    )(preconditioned, store_rows)


def on_device(
    activations,
    out_grads,
    in_projection,
    out_projection,
    inv_curvature,
    store_grads,
    lengths,
    owners,
):
    row_count = lax.axis_size("row")
    mod_count = lax.axis_size("mod")
    queries = lengths.shape[0]
    capacity = 2 * queries // row_count
    feature, placer = featurize(
        activations[0],
        out_grads[0],
        in_projection[0],
        out_projection[0],
        lengths,
        owners,
        capacity,
        row_count * capacity,
    )
    gathered = lax.all_gather(feature, "row", axis=0, tiled=True)
    column_part = precondition(gathered, inv_curvature[0], placer)
    preconditioned = lax.all_gather(column_part, "row", axis=0, tiled=True)
    keep, send = score(preconditioned, store_grads[0], queries, mod_count)
    distance = 1
    while True:
        arrived = lax.ppermute(
            send, "mod", [(i, i ^ distance) for i in range(mod_count)]
        )
        summed = keep + arrived
        distance *= 2
        if distance == mod_count:
            return summed[0]
        keep, send = summed[0::2], summed[1::2]


def solution(mesh):
    return jax.shard_map(
        on_device,
        mesh=mesh,
        in_specs=(
            P("mod", "row", None),
            P("mod", "row", None),
            P("mod", None, None),
            P("mod", None, None),
            P("mod", "row", None),
            P("mod", "row", None),
            P(),
            P(),
        ),
        out_specs=P("mod", "row"),
        check_vma=False,
    )
```

```python
import functools

import jax
import jax.numpy as jnp
from jax import lax
from jax.experimental import pallas as pl
from jax.experimental.pallas import tpu as pltpu
from jax.sharding import PartitionSpec as P

MIB = 1024 * 1024


def contract_last(left, right):
    return lax.dot_general(
        left, right, (((1,), (1,)), ((), ())), preferred_element_type=jnp.float32
    )


def largest_tile(extent, most):
    tile = min(extent, most)
    while extent % tile:
        tile -= 1
    return tile


def split_two(values):
    high = values.astype(jnp.bfloat16)
    return high, (values - high.astype(jnp.float32)).astype(jnp.bfloat16)


def dot(left, right):
    return jnp.dot(left, right, preferred_element_type=jnp.float32)


def chunks_of(units):
    return [(first, min(2, units - first)) for first in range(0, units, 2)]


def featurize_kernel(
    lengths_hbm,
    owners_hbm,
    act_hbm,
    grad_hbm,
    in_proj_hbm,
    out_proj_hbm,
    feature_ref,
    placer_ref,
    act,
    grad,
    in_proj,
    out_proj,
    in_feat,
    out_feat,
    total,
    lengths_ref,
    owners_ref,
    starts,
    stops,
    counts,
    act_sems,
    grad_sems,
    first_sems,
):
    tokens = act.shape[0]
    rank = in_proj.shape[0]
    capacity = feature_ref.shape[0]
    queries, slots = placer_ref.shape
    unit = tokens // capacity
    chunks = chunks_of(capacity)

    def copies(index):
        first, size = chunks[index]
        rows = pl.ds(first * unit, size * unit)
        return (
            pltpu.make_async_copy(act_hbm.at[rows], act.at[rows], act_sems.at[index]),
            pltpu.make_async_copy(grad_hbm.at[rows], grad.at[rows], grad_sems.at[index]),
        )

    first_copies = [
        pltpu.make_async_copy(source, target, first_sems.at[place])
        for place, (source, target) in enumerate(
            (
                (in_proj_hbm, in_proj),
                (out_proj_hbm, out_proj),
                (lengths_hbm, lengths_ref),
                (owners_hbm, owners_ref),
            )
        )
    ]
    for copy in first_copies:
        copy.start()
    for index in range(len(chunks)):
        for copy in copies(index):
            copy.start()

    for copy in first_copies[2:]:
        copy.wait()
    me = lax.axis_index("row")
    for slot in range(capacity):
        starts[slot] = 0
        stops[slot] = 0
    for owner in range(slots // capacity):
        counts[owner] = 0
    used = jnp.int32(0)
    lane = lax.broadcasted_iota(jnp.int32, (1, slots), 1)
    for example in range(queries):
        owner = owners_ref[example]
        length = lengths_ref[example]
        rank_here = counts[owner]
        counts[owner] = rank_here + 1
        mine = owner == me

        @pl.when(mine)
        def _():
            starts[rank_here] = used
            stops[rank_here] = used + length

        used = used + jnp.where(mine, length, 0)
        placer_ref[pl.ds(example, 1), :] = (
            lane == owner * capacity + rank_here
        ).astype(jnp.float32)
    in_feat[pl.ds(0, unit), :] = jnp.zeros((unit, rank), jnp.float32)
    out_feat[:, pl.ds(0, unit)] = jnp.zeros((rank, unit), jnp.float32)

    for copy in first_copies[:2]:
        copy.wait()
    for index, (first, size) in enumerate(chunks):
        for copy in copies(index):
            copy.wait()
        rows = pl.ds(first * unit, size * unit)
        padded = pl.ds((first + 1) * unit, size * unit)
        in_feat[padded, :] = contract_last(act[rows, :], in_proj[...])
        out_feat[:, padded] = contract_last(grad[rows, :], out_proj[...]).T
        for slot in range(first, first + size):
            start, stop = starts[slot], stops[slot]
            window = jnp.maximum((stop + unit - 1) // unit - 1, 0) * unit
            window = pl.multiple_of(window, unit)
            position = (
                window - unit + lax.broadcasted_iota(jnp.int32, (rank, 2 * unit), 1)
            )
            member = (position >= start) & (position < stop)
            out_high, out_low = split_two(
                jnp.where(member, out_feat[:, pl.ds(window, 2 * unit)], 0.0)
            )
            in_high, in_low = split_two(in_feat[pl.ds(window, 2 * unit), :])
            total[pl.ds(slot * rank, rank), :] = (
                dot(out_high, in_high) + dot(out_high, in_low) + dot(out_low, in_high)
            )
    for first in range(0, rank, 2):
        pair = [
            total[pl.ds(first + k, capacity, stride=rank), :] for k in range(2)
        ]
        feature_ref[:, pl.ds(first * rank, 2 * rank)] = jnp.concatenate(
            pair, axis=1
        ).astype(jnp.bfloat16)


def featurize(activations, out_grads, in_projection, out_projection, lengths, owners, capacity, slots):
    tokens, width = activations.shape
    rank = in_projection.shape[0]
    queries = lengths.shape[0]
    unit = tokens // capacity
    chunks = len(chunks_of(capacity))
    return pl.pallas_call(
        featurize_kernel,
        in_specs=[pl.BlockSpec(memory_space=pl.ANY)] * 6,
        out_shape=[
            jax.ShapeDtypeStruct((capacity, rank * rank), jnp.bfloat16),
            jax.ShapeDtypeStruct((queries, slots), jnp.float32),
        ],
        scratch_shapes=[
            pltpu.VMEM((tokens, width), jnp.bfloat16),
            pltpu.VMEM((tokens, width), jnp.bfloat16),
            pltpu.VMEM((rank, width), jnp.bfloat16),
            pltpu.VMEM((rank, width), jnp.bfloat16),
            pltpu.VMEM((unit + tokens, rank), jnp.float32),
            pltpu.VMEM((rank, unit + tokens), jnp.float32),
            pltpu.VMEM((rank * capacity, rank), jnp.float32),
            pltpu.SMEM((queries,), jnp.int32),
            pltpu.SMEM((queries,), jnp.int32),
            pltpu.SMEM((capacity,), jnp.int32),
            pltpu.SMEM((capacity,), jnp.int32),
            pltpu.SMEM((slots // capacity,), jnp.int32),
            pltpu.SemaphoreType.DMA((chunks,)),
            pltpu.SemaphoreType.DMA((chunks,)),
            pltpu.SemaphoreType.DMA((4,)),
        ],
        compiler_params=pltpu.CompilerParams(vmem_limit_bytes=56 * MIB),
        name="featurize",
    )(lengths, owners, activations, out_grads, in_projection, out_projection)


def precondition_kernel(feature_ref, curvature_ref, placer_ref, out_ref, total):
    step = pl.program_id(0)

    @pl.when(step == 0)
    def _():
        total[...] = jnp.zeros_like(total)

    total[...] += contract_last(feature_ref[...], curvature_ref[...])

    @pl.when(step == pl.num_programs(0) - 1)
    def _():
        out_ref[...] = jnp.dot(
            placer_ref[...].astype(jnp.bfloat16),
            total[...].astype(jnp.bfloat16),
            preferred_element_type=jnp.float32,
        ).astype(jnp.bfloat16)


def precondition(gathered, curvature_rows, placer):
    slots, entries = gathered.shape
    columns = curvature_rows.shape[0]
    queries = placer.shape[0]
    depth = largest_tile(entries, 1024)
    return pl.pallas_call(
        precondition_kernel,
        grid=(entries // depth,),
        in_specs=[
            pl.BlockSpec((slots, depth), lambda step: (0, step)),
            pl.BlockSpec((columns, depth), lambda step: (0, step)),
            pl.BlockSpec((queries, slots), lambda step: (0, 0)),
        ],
        out_specs=pl.BlockSpec((queries, columns), lambda step: (0, 0)),
        out_shape=jax.ShapeDtypeStruct((queries, columns), jnp.bfloat16),
        scratch_shapes=[pltpu.VMEM((slots, columns), jnp.float32)],
        compiler_params=pltpu.CompilerParams(vmem_limit_bytes=32 * MIB),
        name="precondition",
    )(gathered, curvature_rows, placer)


def score_kernel(parts, part_ref, store_ref, keep_ref, send_ref, total):
    step = pl.program_id(0)
    share = keep_ref.shape[1]

    @pl.when(step == 0)
    def _():
        total[...] = jnp.zeros_like(total)

    total[...] += contract_last(part_ref[...], store_ref[...])

    @pl.when(step == pl.num_programs(0) - 1)
    def _():
        me = lax.axis_index("mod")
        for place in range(parts):
            row = pl.multiple_of((me ^ place) * share, share)
            block = total[pl.ds(row, share), :]
            if place % 2:
                send_ref[place // 2] = block
            else:
                keep_ref[place // 2] = block


def score(preconditioned, store_rows, queries, parts):
    stores, entries = store_rows.shape
    depth = preconditioned.shape[1]
    share = queries // parts
    half = jax.ShapeDtypeStruct((parts // 2, share, stores), jnp.float32)
    half_spec = pl.BlockSpec((parts // 2, share, stores), lambda step: (0, 0, 0))
    return pl.pallas_call(
        functools.partial(score_kernel, parts),
        grid=(entries // depth,),
        in_specs=[
            pl.BlockSpec((queries, depth), lambda step: (step, 0)),
            pl.BlockSpec((stores, depth), lambda step: (0, step)),
        ],
        out_specs=[half_spec, half_spec],
        out_shape=[half, half],
        scratch_shapes=[pltpu.VMEM((queries, stores), jnp.float32)],
        compiler_params=pltpu.CompilerParams(vmem_limit_bytes=32 * MIB),
        name="score",
    )(preconditioned, store_rows)


def on_device(
    activations,
    out_grads,
    in_projection,
    out_projection,
    inv_curvature,
    store_grads,
    lengths,
    owners,
):
    row_count = lax.axis_size("row")
    mod_count = lax.axis_size("mod")
    queries = lengths.shape[0]
    capacity = 2 * queries // row_count
    feature, placer = featurize(
        activations[0],
        out_grads[0],
        in_projection[0],
        out_projection[0],
        lengths,
        owners,
        capacity,
        row_count * capacity,
    )
    gathered = lax.all_gather(feature, "row", axis=0, tiled=True)
    column_part = precondition(gathered, inv_curvature[0], placer)
    preconditioned = lax.all_gather(column_part, "row", axis=0, tiled=True)
    keep, send = score(preconditioned, store_grads[0], queries, mod_count)
    distance = 1
    while True:
        arrived = lax.ppermute(
            send, "mod", [(i, i ^ distance) for i in range(mod_count)]
        )
        summed = keep + arrived
        distance *= 2
        if distance == mod_count:
            return summed[0]
        keep, send = summed[0::2], summed[1::2]


def solution(mesh):
    return jax.shard_map(
        on_device,
        mesh=mesh,
        in_specs=(
            P("mod", "row", None),
            P("mod", "row", None),
            P("mod", None, None),
            P("mod", None, None),
            P("mod", "row", None),
            P("mod", "row", None),
            P(),
            P(),
        ),
        out_specs=P("mod", "row"),
        check_vma=False,
    )
```

```python
import functools

import jax
import jax.numpy as jnp
from jax import lax
from jax.experimental import pallas as pl
from jax.experimental.pallas import tpu as pltpu
from jax.sharding import PartitionSpec as P

MIB = 1024 * 1024


def contract_last(left, right):
    return lax.dot_general(
        left, right, (((1,), (1,)), ((), ())), preferred_element_type=jnp.float32
    )


def split_two(values):
    high = values.astype(jnp.bfloat16)
    return high, (values - high.astype(jnp.float32)).astype(jnp.bfloat16)


def dot(left, right):
    return jnp.dot(left, right, preferred_element_type=jnp.float32)


def chunks_of(units):
    return [(first, min(2, units - first)) for first in range(0, units, 2)]


def featurize_kernel(
    lengths_hbm,
    owners_hbm,
    curvature_hbm,
    act_hbm,
    grad_hbm,
    in_proj_hbm,
    out_proj_hbm,
    feature_ref,
    placer_ref,
    curvature_ref,
    act,
    grad,
    in_proj,
    out_proj,
    in_feat,
    out_feat,
    total,
    lengths_ref,
    owners_ref,
    starts,
    stops,
    counts,
    act_sems,
    grad_sems,
    first_sems,
):
    tokens = act.shape[0]
    rank = in_proj.shape[0]
    capacity = feature_ref.shape[0]
    queries, slots = placer_ref.shape
    unit = tokens // capacity
    chunks = chunks_of(capacity)

    def copies(index):
        first, size = chunks[index]
        rows = pl.ds(first * unit, size * unit)
        return (
            pltpu.make_async_copy(act_hbm.at[rows], act.at[rows], act_sems.at[index]),
            pltpu.make_async_copy(grad_hbm.at[rows], grad.at[rows], grad_sems.at[index]),
        )

    first_copies = [
        pltpu.make_async_copy(source, target, first_sems.at[place])
        for place, (source, target) in enumerate(
            (
                (in_proj_hbm, in_proj),
                (out_proj_hbm, out_proj),
                (lengths_hbm, lengths_ref),
                (owners_hbm, owners_ref),
            )
        )
    ]
    for copy in first_copies:
        copy.start()
    for index in range(len(chunks)):
        for copy in copies(index):
            copy.start()

    curvature_copy = pltpu.make_async_copy(curvature_hbm, curvature_ref, first_sems.at[4])
    curvature_copy.start()

    for copy in first_copies[2:]:
        copy.wait()
    me = lax.axis_index("row")
    for slot in range(capacity):
        starts[slot] = 0
        stops[slot] = 0
    for owner in range(slots // capacity):
        counts[owner] = 0
    used = jnp.int32(0)
    lane = lax.broadcasted_iota(jnp.int32, (1, slots), 1)
    for example in range(queries):
        owner = owners_ref[example]
        length = lengths_ref[example]
        rank_here = counts[owner]
        counts[owner] = rank_here + 1
        mine = owner == me

        @pl.when(mine)
        def _():
            starts[rank_here] = used
            stops[rank_here] = used + length

        used = used + jnp.where(mine, length, 0)
        placer_ref[pl.ds(example, 1), :] = (
            lane == owner * capacity + rank_here
        ).astype(jnp.float32)
    in_feat[pl.ds(0, unit), :] = jnp.zeros((unit, rank), jnp.float32)
    out_feat[:, pl.ds(0, unit)] = jnp.zeros((rank, unit), jnp.float32)

    for copy in first_copies[:2]:
        copy.wait()
    for index, (first, size) in enumerate(chunks):
        for copy in copies(index):
            copy.wait()
        rows = pl.ds(first * unit, size * unit)
        padded = pl.ds((first + 1) * unit, size * unit)
        in_feat[padded, :] = contract_last(act[rows, :], in_proj[...])
        out_feat[:, padded] = contract_last(grad[rows, :], out_proj[...]).T
    for slot in range(capacity):
        start, stop = starts[slot], stops[slot]
        window = jnp.maximum((stop + unit - 1) // unit - 1, 0) * unit
        window = pl.multiple_of(window, unit)
        position = (
            window - unit + lax.broadcasted_iota(jnp.int32, (rank, 2 * unit), 1)
        )
        member = (position >= start) & (position < stop)
        out_high, out_low = split_two(
            jnp.where(member, out_feat[:, pl.ds(window, 2 * unit)], 0.0)
        )
        in_high, in_low = split_two(in_feat[pl.ds(window, 2 * unit), :])
        total[pl.ds(slot * rank, rank), :] = (
            dot(out_high, in_high) + dot(out_high, in_low) + dot(out_low, in_high)
        )
    for first in range(0, rank, 2):
        pair = [
            total[pl.ds(first + k, capacity, stride=rank), :] for k in range(2)
        ]
        feature_ref[:, pl.ds(first * rank, 2 * rank)] = jnp.concatenate(
            pair, axis=1
        ).astype(jnp.bfloat16)
    curvature_copy.wait()


def featurize(
    activations, out_grads, in_projection, out_projection, curvature, lengths, owners, capacity, slots
):
    tokens, width = activations.shape
    rank = in_projection.shape[0]
    queries = lengths.shape[0]
    unit = tokens // capacity
    chunks = len(chunks_of(capacity))
    return pl.pallas_call(
        featurize_kernel,
        in_specs=[pl.BlockSpec(memory_space=pl.ANY)] * 7,
        out_shape=[
            pltpu.VMEM((capacity, rank * rank), jnp.bfloat16),
            pltpu.VMEM((queries, slots), jnp.float32),
            pltpu.VMEM(curvature.shape, curvature.dtype),
        ],
        out_specs=[pl.BlockSpec(memory_space=pltpu.VMEM)] * 3,
        scratch_shapes=[
            pltpu.VMEM((tokens, width), jnp.bfloat16),
            pltpu.VMEM((tokens, width), jnp.bfloat16),
            pltpu.VMEM((rank, width), jnp.bfloat16),
            pltpu.VMEM((rank, width), jnp.bfloat16),
            pltpu.VMEM((unit + tokens, rank), jnp.float32),
            pltpu.VMEM((rank, unit + tokens), jnp.float32),
            pltpu.VMEM((rank * capacity, rank), jnp.float32),
            pltpu.SMEM((queries,), jnp.int32),
            pltpu.SMEM((queries,), jnp.int32),
            pltpu.SMEM((capacity,), jnp.int32),
            pltpu.SMEM((capacity,), jnp.int32),
            pltpu.SMEM((slots // capacity,), jnp.int32),
            pltpu.SemaphoreType.DMA((chunks,)),
            pltpu.SemaphoreType.DMA((chunks,)),
            pltpu.SemaphoreType.DMA((5,)),
        ],
        compiler_params=pltpu.CompilerParams(vmem_limit_bytes=51 * MIB),
        name="featurize",
    )(lengths, owners, curvature, activations, out_grads, in_projection, out_projection)


def precondition_kernel(feature_ref, curvature_ref, placer_ref, out_ref):
    by_slot = contract_last(feature_ref[...], curvature_ref[...]).astype(jnp.bfloat16)
    out_ref[...] = dot(placer_ref[...].astype(jnp.bfloat16), by_slot).astype(jnp.bfloat16)


def precondition(gathered, curvature_rows, placer):
    return pl.pallas_call(
        precondition_kernel,
        in_specs=[pl.BlockSpec(memory_space=pltpu.VMEM)] * 3,
        out_specs=pl.BlockSpec(memory_space=pltpu.VMEM),
        out_shape=jax.ShapeDtypeStruct((placer.shape[0], curvature_rows.shape[0]), jnp.bfloat16),
        compiler_params=pltpu.CompilerParams(vmem_limit_bytes=16 * MIB),
        name="precondition",
    )(gathered, curvature_rows, placer)


def score_kernel(parts, part_ref, store_ref, keep_ref, send_ref, total):
    share = keep_ref.shape[1]
    queries, stores = total.shape
    depth = part_ref.shape[1]
    scores = jnp.zeros((queries, stores), jnp.float32)
    for block in range(part_ref.shape[0] // queries):
        scores += contract_last(
            part_ref[pl.ds(block * queries, queries), :],
            store_ref[:, pl.ds(block * depth, depth)],
        )
    total[...] = scores
    me = lax.axis_index("mod")
    for place in range(parts):
        row = pl.multiple_of((me ^ place) * share, share)
        block = total[pl.ds(row, share), :]
        if place % 2:
            send_ref[place // 2] = block
        else:
            keep_ref[place // 2] = block


def score(preconditioned, store_rows, queries, parts):
    stores = store_rows.shape[0]
    half = jax.ShapeDtypeStruct((parts // 2, queries // parts, stores), jnp.float32)
    return pl.pallas_call(
        functools.partial(score_kernel, parts),
        in_specs=[pl.BlockSpec(memory_space=pltpu.VMEM)] * 2,
        out_specs=[pl.BlockSpec(memory_space=pltpu.VMEM)] * 2,
        out_shape=[half, half],
        scratch_shapes=[pltpu.VMEM((queries, stores), jnp.float32)],
        compiler_params=pltpu.CompilerParams(vmem_limit_bytes=16 * MIB),
        name="score",
    )(preconditioned, store_rows)


def on_device(
    activations,
    out_grads,
    in_projection,
    out_projection,
    inv_curvature,
    store_grads,
    lengths,
    owners,
):
    row_count = lax.axis_size("row")
    mod_count = lax.axis_size("mod")
    queries = lengths.shape[0]
    capacity = 2 * queries // row_count
    feature, placer, curvature = featurize(
        activations[0],
        out_grads[0],
        in_projection[0],
        out_projection[0],
        inv_curvature[0],
        lengths,
        owners,
        capacity,
        row_count * capacity,
    )
    gathered = lax.all_gather(feature, "row", axis=0, tiled=True)
    column_part = precondition(gathered, curvature, placer)
    preconditioned = lax.all_gather(column_part, "row", axis=0, tiled=True)
    keep, send = score(preconditioned, store_grads[0], queries, mod_count)
    distance = 1
    while True:
        arrived = lax.ppermute(
            send, "mod", [(i, i ^ distance) for i in range(mod_count)]
        )
        summed = keep + arrived
        distance *= 2
        if distance == mod_count:
            return summed[0]
        keep, send = summed[0::2], summed[1::2]


def solution(mesh):
    return jax.shard_map(
        on_device,
        mesh=mesh,
        in_specs=(
            P("mod", "row", None),
            P("mod", "row", None),
            P("mod", None, None),
            P("mod", None, None),
            P("mod", "row", None),
            P("mod", "row", None),
            P(),
            P(),
        ),
        out_specs=P("mod", "row"),
        check_vma=False,
    )
```

```python
import functools

import jax
import jax.numpy as jnp
from jax import lax
from jax.experimental import pallas as pl
from jax.experimental.pallas import tpu as pltpu
from jax.sharding import PartitionSpec as P

MIB = 1024 * 1024


def contract_last(left, right):
    return lax.dot_general(
        left, right, (((1,), (1,)), ((), ())), preferred_element_type=jnp.float32
    )


def split_two(values):
    high = values.astype(jnp.bfloat16)
    return high, (values - high.astype(jnp.float32)).astype(jnp.bfloat16)


def dot(left, right):
    return jnp.dot(left, right, preferred_element_type=jnp.float32)


def chunks_of(units):
    return [(first, min(2, units - first)) for first in range(0, units, 2)]


def featurize_kernel(
    lengths_hbm,
    owners_hbm,
    curvature_hbm,
    act_hbm,
    grad_hbm,
    in_proj_hbm,
    out_proj_hbm,
    feature_ref,
    placer_ref,
    curvature_ref,
    act,
    grad,
    in_proj,
    out_proj,
    in_feat,
    out_feat,
    total,
    lengths_ref,
    owners_ref,
    starts,
    stops,
    counts,
    act_sems,
    grad_sems,
    first_sems,
):
    tokens = act.shape[0]
    rank = in_proj.shape[0]
    capacity = feature_ref.shape[0]
    queries, slots = placer_ref.shape
    unit = tokens // capacity
    chunks = chunks_of(capacity)

    def copies(index):
        first, size = chunks[index]
        rows = pl.ds(first * unit, size * unit)
        return (
            pltpu.make_async_copy(act_hbm.at[rows], act.at[rows], act_sems.at[index]),
            pltpu.make_async_copy(grad_hbm.at[rows], grad.at[rows], grad_sems.at[index]),
        )

    first_copies = [
        pltpu.make_async_copy(source, target, first_sems.at[place])
        for place, (source, target) in enumerate(
            (
                (in_proj_hbm, in_proj),
                (out_proj_hbm, out_proj),
                (lengths_hbm, lengths_ref),
                (owners_hbm, owners_ref),
            )
        )
    ]
    for copy in first_copies:
        copy.start()
    for index in range(len(chunks)):
        for copy in copies(index):
            copy.start()

    curvature_copy = pltpu.make_async_copy(curvature_hbm, curvature_ref, first_sems.at[4])
    curvature_copy.start()

    for copy in first_copies[2:]:
        copy.wait()
    me = lax.axis_index("row")
    for slot in range(capacity):
        starts[slot] = 0
        stops[slot] = 0
    for owner in range(slots // capacity):
        counts[owner] = 0
    used = jnp.int32(0)
    lane = lax.broadcasted_iota(jnp.int32, (1, slots), 1)
    for example in range(queries):
        owner = owners_ref[example]
        length = lengths_ref[example]
        rank_here = counts[owner]
        counts[owner] = rank_here + 1
        mine = owner == me

        @pl.when(mine)
        def _():
            starts[rank_here] = used
            stops[rank_here] = used + length

        used = used + jnp.where(mine, length, 0)
        placer_ref[pl.ds(example, 1), :] = (
            lane == (owner ^ me) * capacity + rank_here
        ).astype(jnp.float32)
    in_feat[pl.ds(0, unit), :] = jnp.zeros((unit, rank), jnp.float32)
    out_feat[:, pl.ds(0, unit)] = jnp.zeros((rank, unit), jnp.float32)

    for copy in first_copies[:2]:
        copy.wait()
    for index, (first, size) in enumerate(chunks):
        for copy in copies(index):
            copy.wait()
        rows = pl.ds(first * unit, size * unit)
        padded = pl.ds((first + 1) * unit, size * unit)
        in_feat[padded, :] = contract_last(act[rows, :], in_proj[...])
        out_feat[:, padded] = contract_last(grad[rows, :], out_proj[...]).T
    for slot in range(capacity):
        start, stop = starts[slot], stops[slot]
        window = jnp.maximum((stop + unit - 1) // unit - 1, 0) * unit
        window = pl.multiple_of(window, unit)
        position = (
            window - unit + lax.broadcasted_iota(jnp.int32, (rank, 2 * unit), 1)
        )
        member = (position >= start) & (position < stop)
        out_high, out_low = split_two(
            jnp.where(member, out_feat[:, pl.ds(window, 2 * unit)], 0.0)
        )
        in_high, in_low = split_two(in_feat[pl.ds(window, 2 * unit), :])
        total[pl.ds(slot * rank, rank), :] = (
            dot(out_high, in_high) + dot(out_high, in_low) + dot(out_low, in_high)
        )
    for first in range(0, rank, 2):
        pair = [
            total[pl.ds(first + k, capacity, stride=rank), :] for k in range(2)
        ]
        feature_ref[:, pl.ds(first * rank, 2 * rank)] = jnp.concatenate(
            pair, axis=1
        ).astype(jnp.bfloat16)
    curvature_copy.wait()


def featurize(
    activations, out_grads, in_projection, out_projection, curvature, lengths, owners, capacity, slots
):
    tokens, width = activations.shape
    rank = in_projection.shape[0]
    queries = lengths.shape[0]
    unit = tokens // capacity
    chunks = len(chunks_of(capacity))
    return pl.pallas_call(
        featurize_kernel,
        in_specs=[pl.BlockSpec(memory_space=pl.ANY)] * 7,
        out_shape=[
            pltpu.VMEM((capacity, rank * rank), jnp.bfloat16),
            pltpu.VMEM((queries, slots), jnp.float32),
            pltpu.VMEM(curvature.shape, curvature.dtype),
        ],
        out_specs=[pl.BlockSpec(memory_space=pltpu.VMEM)] * 3,
        scratch_shapes=[
            pltpu.VMEM((tokens, width), jnp.bfloat16),
            pltpu.VMEM((tokens, width), jnp.bfloat16),
            pltpu.VMEM((rank, width), jnp.bfloat16),
            pltpu.VMEM((rank, width), jnp.bfloat16),
            pltpu.VMEM((unit + tokens, rank), jnp.float32),
            pltpu.VMEM((rank, unit + tokens), jnp.float32),
            pltpu.VMEM((rank * capacity, rank), jnp.float32),
            pltpu.SMEM((queries,), jnp.int32),
            pltpu.SMEM((queries,), jnp.int32),
            pltpu.SMEM((capacity,), jnp.int32),
            pltpu.SMEM((capacity,), jnp.int32),
            pltpu.SMEM((slots // capacity,), jnp.int32),
            pltpu.SemaphoreType.DMA((chunks,)),
            pltpu.SemaphoreType.DMA((chunks,)),
            pltpu.SemaphoreType.DMA((5,)),
        ],
        compiler_params=pltpu.CompilerParams(vmem_limit_bytes=51 * MIB),
        name="featurize",
    )(lengths, owners, curvature, activations, out_grads, in_projection, out_projection)


def precondition_kernel(curvature_ref, placer_ref, *rest):
    piece_refs, out_ref, feature = rest[:-2], rest[-2], rest[-1]
    capacity = piece_refs[0].shape[0]
    for place, piece_ref in enumerate(piece_refs):
        feature[pl.ds(place * capacity, capacity), :] = piece_ref[...]
    by_slot = contract_last(feature[...], curvature_ref[...]).astype(jnp.bfloat16)
    out_ref[...] = dot(placer_ref[...].astype(jnp.bfloat16), by_slot).astype(jnp.bfloat16)


def precondition(pieces, curvature_rows, placer):
    capacity, entries = pieces[0].shape
    return pl.pallas_call(
        precondition_kernel,
        in_specs=[pl.BlockSpec(memory_space=pltpu.VMEM)] * (2 + len(pieces)),
        out_specs=pl.BlockSpec(memory_space=pltpu.VMEM),
        out_shape=pltpu.VMEM((placer.shape[0], curvature_rows.shape[0]), jnp.bfloat16),
        scratch_shapes=[pltpu.VMEM((len(pieces) * capacity, entries), jnp.bfloat16)],
        compiler_params=pltpu.CompilerParams(vmem_limit_bytes=16 * MIB),
        name="precondition",
    )(curvature_rows, placer, *pieces)


def score_kernel(parts, store_ref, *rest):
    piece_refs = rest[: -parts - 1]
    share_refs, total = rest[-parts - 1 : -1], rest[-1]
    share = share_refs[0].shape[0]
    queries, stores = total.shape
    depth = piece_refs[0].shape[1]
    column = lax.axis_index("row")
    scores = jnp.zeros((queries, stores), jnp.float32)
    for place, piece_ref in enumerate(piece_refs):
        first = pl.multiple_of((column ^ place) * depth, depth)
        scores += contract_last(piece_ref[...], store_ref[:, pl.ds(first, depth)])
    total[...] = scores
    me = lax.axis_index("mod")
    for place in range(parts):
        row = pl.multiple_of((me ^ place) * share, share)
        share_refs[place][...] = total[pl.ds(row, share), :]


def score(pieces, store_rows, queries, parts):
    stores = store_rows.shape[0]
    one = pltpu.VMEM((queries // parts, stores), jnp.float32)
    return pl.pallas_call(
        functools.partial(score_kernel, parts),
        in_specs=[pl.BlockSpec(memory_space=pltpu.VMEM)] * (1 + len(pieces)),
        out_specs=[pl.BlockSpec(memory_space=pltpu.VMEM)] * parts,
        out_shape=[one] * parts,
        scratch_shapes=[pltpu.VMEM((queries, stores), jnp.float32)],
        compiler_params=pltpu.CompilerParams(vmem_limit_bytes=16 * MIB),
        name="score",
    )(store_rows, *pieces)


def exchange(array, axis, distance):
    count = lax.axis_size(axis)
    return lax.ppermute(array, axis, [(i, i ^ distance) for i in range(count)])


def pieces_of_all(mine, axis):
    count = lax.axis_size(axis)
    far = {0: mine}
    for d in sorted(range(2, count, 2), key=lambda d: -bin(d).count("1")):
        far[d] = exchange(mine, axis, d)
    pieces = []
    for d in range(0, count, 2):
        pieces += [far[d], exchange(far[d], axis, 1)]
    return pieces


def on_device(
    activations,
    out_grads,
    in_projection,
    out_projection,
    inv_curvature,
    store_grads,
    lengths,
    owners,
):
    row_count = lax.axis_size("row")
    mod_count = lax.axis_size("mod")
    queries = lengths.shape[0]
    capacity = 2 * queries // row_count
    feature, placer, curvature = featurize(
        activations[0],
        out_grads[0],
        in_projection[0],
        out_projection[0],
        inv_curvature[0],
        lengths,
        owners,
        capacity,
        row_count * capacity,
    )
    column_part = precondition(pieces_of_all(feature, "row"), curvature, placer)
    shares = score(pieces_of_all(column_part, "row"), store_grads[0], queries, mod_count)
    total = shares[0]
    for d in reversed(range(1, mod_count)):
        total = total + exchange(shares[d], "mod", d)
    return total


def solution(mesh):
    return jax.shard_map(
        on_device,
        mesh=mesh,
        in_specs=(
            P("mod", "row", None),
            P("mod", "row", None),
            P("mod", None, None),
            P("mod", None, None),
            P("mod", "row", None),
            P("mod", "row", None),
            P(),
            P(),
        ),
        out_specs=P("mod", "row"),
        check_vma=False,
    )
```

```python
import functools

import jax
import jax.numpy as jnp
from jax import lax
from jax.experimental import pallas as pl
from jax.experimental.pallas import tpu as pltpu
from jax.sharding import PartitionSpec as P

MIB = 1024 * 1024


def contract_last(left, right):
    return lax.dot_general(
        left, right, (((1,), (1,)), ((), ())), preferred_element_type=jnp.float32
    )


def ring_member(place):
    return place ^ (place >> 1)


def ring_place(member):
    place = member
    for shift in (1, 2, 4):
        place = place ^ (place >> shift)
    return place


def split_two(values):
    high = values.astype(jnp.bfloat16)
    return high, (values - high.astype(jnp.float32)).astype(jnp.bfloat16)


def dot(left, right):
    return jnp.dot(left, right, preferred_element_type=jnp.float32)


def chunks_of(units):
    return [(first, min(2, units - first)) for first in range(0, units, 2)]


def featurize_kernel(
    lengths_hbm,
    owners_hbm,
    curvature_hbm,
    act_hbm,
    grad_hbm,
    in_proj_hbm,
    out_proj_hbm,
    feature_ref,
    placer_ref,
    curvature_ref,
    act,
    grad,
    in_proj,
    out_proj,
    in_feat,
    out_feat,
    total,
    lengths_ref,
    owners_ref,
    starts,
    stops,
    counts,
    act_sems,
    grad_sems,
    first_sems,
):
    tokens = act.shape[0]
    rank = in_proj.shape[0]
    capacity = feature_ref.shape[0]
    queries, slots = placer_ref.shape
    unit = tokens // capacity
    chunks = chunks_of(capacity)

    def copies(index):
        first, size = chunks[index]
        rows = pl.ds(first * unit, size * unit)
        return (
            pltpu.make_async_copy(act_hbm.at[rows], act.at[rows], act_sems.at[index]),
            pltpu.make_async_copy(grad_hbm.at[rows], grad.at[rows], grad_sems.at[index]),
        )

    first_copies = [
        pltpu.make_async_copy(source, target, first_sems.at[place])
        for place, (source, target) in enumerate(
            (
                (in_proj_hbm, in_proj),
                (out_proj_hbm, out_proj),
                (lengths_hbm, lengths_ref),
                (owners_hbm, owners_ref),
            )
        )
    ]
    for copy in first_copies:
        copy.start()
    for index in range(len(chunks)):
        for copy in copies(index):
            copy.start()

    curvature_copy = pltpu.make_async_copy(curvature_hbm, curvature_ref, first_sems.at[4])
    curvature_copy.start()

    for copy in first_copies[2:]:
        copy.wait()
    me = lax.axis_index("row")
    for slot in range(capacity):
        starts[slot] = 0
        stops[slot] = 0
    for owner in range(slots // capacity):
        counts[owner] = 0
    used = jnp.int32(0)
    lane = lax.broadcasted_iota(jnp.int32, (1, slots), 1)
    for example in range(queries):
        owner = owners_ref[example]
        length = lengths_ref[example]
        rank_here = counts[owner]
        counts[owner] = rank_here + 1
        mine = owner == me

        @pl.when(mine)
        def _():
            starts[rank_here] = used
            stops[rank_here] = used + length

        used = used + jnp.where(mine, length, 0)
        placer_ref[pl.ds(example, 1), :] = (
            lane == (owner ^ me) * capacity + rank_here
        ).astype(jnp.float32)
    in_feat[pl.ds(0, unit), :] = jnp.zeros((unit, rank), jnp.float32)
    out_feat[:, pl.ds(0, unit)] = jnp.zeros((rank, unit), jnp.float32)

    for copy in first_copies[:2]:
        copy.wait()
    for index, (first, size) in enumerate(chunks):
        for copy in copies(index):
            copy.wait()
        rows = pl.ds(first * unit, size * unit)
        padded = pl.ds((first + 1) * unit, size * unit)
        in_feat[padded, :] = contract_last(act[rows, :], in_proj[...])
        out_feat[:, padded] = contract_last(grad[rows, :], out_proj[...]).T
    for slot in range(capacity):
        start, stop = starts[slot], stops[slot]
        window = jnp.maximum((stop + unit - 1) // unit - 1, 0) * unit
        window = pl.multiple_of(window, unit)
        position = (
            window - unit + lax.broadcasted_iota(jnp.int32, (rank, 2 * unit), 1)
        )
        member = (position >= start) & (position < stop)
        out_high, out_low = split_two(
            jnp.where(member, out_feat[:, pl.ds(window, 2 * unit)], 0.0)
        )
        in_high, in_low = split_two(in_feat[pl.ds(window, 2 * unit), :])
        total[pl.ds(slot * rank, rank), :] = (
            dot(out_high, in_high) + dot(out_high, in_low) + dot(out_low, in_high)
        )
    for first in range(0, rank, 2):
        pair = [
            total[pl.ds(first + k, capacity, stride=rank), :] for k in range(2)
        ]
        feature_ref[:, pl.ds(first * rank, 2 * rank)] = jnp.concatenate(
            pair, axis=1
        ).astype(jnp.bfloat16)
    curvature_copy.wait()


def featurize(
    activations, out_grads, in_projection, out_projection, curvature, lengths, owners, capacity, slots
):
    tokens, width = activations.shape
    rank = in_projection.shape[0]
    queries = lengths.shape[0]
    unit = tokens // capacity
    chunks = len(chunks_of(capacity))
    return pl.pallas_call(
        featurize_kernel,
        in_specs=[pl.BlockSpec(memory_space=pl.ANY)] * 7,
        out_shape=[
            pltpu.VMEM((capacity, rank * rank), jnp.bfloat16),
            pltpu.VMEM((queries, slots), jnp.float32),
            pltpu.VMEM(curvature.shape, curvature.dtype),
        ],
        out_specs=[pl.BlockSpec(memory_space=pltpu.VMEM)] * 3,
        scratch_shapes=[
            pltpu.VMEM((tokens, width), jnp.bfloat16),
            pltpu.VMEM((tokens, width), jnp.bfloat16),
            pltpu.VMEM((rank, width), jnp.bfloat16),
            pltpu.VMEM((rank, width), jnp.bfloat16),
            pltpu.VMEM((unit + tokens, rank), jnp.float32),
            pltpu.VMEM((rank, unit + tokens), jnp.float32),
            pltpu.VMEM((rank * capacity, rank), jnp.float32),
            pltpu.SMEM((queries,), jnp.int32),
            pltpu.SMEM((queries,), jnp.int32),
            pltpu.SMEM((capacity,), jnp.int32),
            pltpu.SMEM((capacity,), jnp.int32),
            pltpu.SMEM((slots // capacity,), jnp.int32),
            pltpu.SemaphoreType.DMA((chunks,)),
            pltpu.SemaphoreType.DMA((chunks,)),
            pltpu.SemaphoreType.DMA((5,)),
        ],
        compiler_params=pltpu.CompilerParams(vmem_limit_bytes=51 * MIB),
        name="featurize",
    )(lengths, owners, curvature, activations, out_grads, in_projection, out_projection)


def precondition_kernel(curvature_ref, placer_ref, *rest):
    piece_refs, out_ref, feature = rest[:-2], rest[-2], rest[-1]
    capacity = piece_refs[0].shape[0]
    for place, piece_ref in enumerate(piece_refs):
        feature[pl.ds(place * capacity, capacity), :] = piece_ref[...]
    by_slot = contract_last(feature[...], curvature_ref[...]).astype(jnp.bfloat16)
    out_ref[...] = dot(placer_ref[...].astype(jnp.bfloat16), by_slot).astype(jnp.bfloat16)


def precondition(pieces, curvature_rows, placer):
    capacity, entries = pieces[0].shape
    return pl.pallas_call(
        precondition_kernel,
        in_specs=[pl.BlockSpec(memory_space=pltpu.VMEM)] * (2 + len(pieces)),
        out_specs=pl.BlockSpec(memory_space=pltpu.VMEM),
        out_shape=pltpu.VMEM((placer.shape[0], curvature_rows.shape[0]), jnp.bfloat16),
        scratch_shapes=[pltpu.VMEM((len(pieces) * capacity, entries), jnp.bfloat16)],
        compiler_params=pltpu.CompilerParams(vmem_limit_bytes=16 * MIB),
        name="precondition",
    )(curvature_rows, placer, *pieces)


def partial_scores(places, store_ref, piece_refs):
    queries, depth = piece_refs[0].shape
    column = lax.axis_index("row")
    scores = jnp.zeros((store_ref.shape[0], queries), jnp.float32)
    for place, piece_ref in zip(places, piece_refs):
        first = pl.multiple_of((column ^ place) * depth, depth)
        scores += contract_last(store_ref[:, pl.ds(first, depth)], piece_ref[...])
    return scores


def early_score_kernel(places, store_ref, *rest):
    rest[-1][...] = partial_scores(places, store_ref, rest[:-1])


def score_kernel(places, parts, early_ref, store_ref, *rest):
    piece_refs = rest[: -parts - 1]
    share_refs, total = rest[-parts - 1 : -1], rest[-1]
    share = share_refs[0].shape[0]
    total[...] = (early_ref[...] + partial_scores(places, store_ref, piece_refs)).T
    me = lax.axis_index("mod")
    for place in range(parts):
        member = ring_member(lax.rem(ring_place(me) + place, parts))
        row = pl.multiple_of(member * share, share)
        share_refs[place][...] = total[pl.ds(row, share), :]


def score(pieces, store_rows, queries, parts, early_places):
    stores = store_rows.shape[0]
    late_places = [d for d in range(len(pieces)) if d not in early_places]
    early = pl.pallas_call(
        functools.partial(early_score_kernel, early_places),
        in_specs=[pl.BlockSpec(memory_space=pltpu.VMEM)] * (1 + len(early_places)),
        out_specs=pl.BlockSpec(memory_space=pltpu.VMEM),
        out_shape=pltpu.VMEM((stores, queries), jnp.float32),
        compiler_params=pltpu.CompilerParams(vmem_limit_bytes=16 * MIB),
        name="early_score",
    )(store_rows, *[pieces[d] for d in early_places])
    one = pltpu.VMEM((queries // parts, stores), jnp.float32)
    return pl.pallas_call(
        functools.partial(score_kernel, late_places, parts),
        in_specs=[pl.BlockSpec(memory_space=pltpu.VMEM)] * (2 + len(late_places)),
        out_specs=[pl.BlockSpec(memory_space=pltpu.VMEM)] * parts,
        out_shape=[one] * parts,
        scratch_shapes=[pltpu.VMEM((queries, stores), jnp.float32)],
        compiler_params=pltpu.CompilerParams(vmem_limit_bytes=16 * MIB),
        name="score",
    )(early, store_rows, *[pieces[d] for d in late_places])


def exchange(array, axis, distance):
    count = lax.axis_size(axis)
    return lax.ppermute(array, axis, [(i, i ^ distance) for i in range(count)])


def send_on(array, axis, places):
    count = lax.axis_size(axis)
    order = [ring_member(place) for place in range(count)]
    return lax.ppermute(
        array, axis, [(order[i], order[(i + places) % count]) for i in range(count)]
    )


def pieces_of_all(mine, axis):
    count = lax.axis_size(axis)
    far = {0: mine}
    for d in sorted(range(2, count, 2), key=lambda d: -bin(d).count("1")):
        far[d] = exchange(mine, axis, d)
    pieces = []
    for d in range(0, count, 2):
        pieces += [far[d], exchange(far[d], axis, 1)]
    return pieces


def on_device(
    activations,
    out_grads,
    in_projection,
    out_projection,
    inv_curvature,
    store_grads,
    lengths,
    owners,
):
    row_count = lax.axis_size("row")
    mod_count = lax.axis_size("mod")
    queries = lengths.shape[0]
    capacity = 2 * queries // row_count
    feature, placer, curvature = featurize(
        activations[0],
        out_grads[0],
        in_projection[0],
        out_projection[0],
        inv_curvature[0],
        lengths,
        owners,
        capacity,
        row_count * capacity,
    )
    column_part = precondition(pieces_of_all(feature, "row"), curvature, placer)
    shares = score(pieces_of_all(column_part, "row"), store_grads[0], queries, mod_count, [0, 1])
    total = shares[0]
    for places in range(1, mod_count):
        total = total + send_on(shares[places], "mod", places)
    return total


def solution(mesh):
    return jax.shard_map(
        on_device,
        mesh=mesh,
        in_specs=(
            P("mod", "row", None),
            P("mod", "row", None),
            P("mod", None, None),
            P("mod", None, None),
            P("mod", "row", None),
            P("mod", "row", None),
            P(),
            P(),
        ),
        out_specs=P("mod", "row"),
        check_vma=False,
    )
```

```python
import functools

import jax
import jax.numpy as jnp
from jax import lax
from jax.experimental import pallas as pl
from jax.experimental.pallas import tpu as pltpu
from jax.sharding import PartitionSpec as P

MIB = 1024 * 1024


def contract_last(left, right):
    return lax.dot_general(
        left, right, (((1,), (1,)), ((), ())), preferred_element_type=jnp.float32
    )


def ring_member(place):
    return place ^ (place >> 1)


def ring_place(member):
    place = member
    for shift in (1, 2, 4):
        place = place ^ (place >> shift)
    return place


def split_two(values):
    high = values.astype(jnp.bfloat16)
    return high, (values - high.astype(jnp.float32)).astype(jnp.bfloat16)


def dot(left, right):
    return jnp.dot(left, right, preferred_element_type=jnp.float32)


def chunks_of(units):
    return [(first, min(2, units - first)) for first in range(0, units, 2)]


def featurize_kernel(
    lengths_hbm,
    owners_hbm,
    curvature_hbm,
    act_hbm,
    grad_hbm,
    in_proj_hbm,
    out_proj_hbm,
    feature_ref,
    placer_ref,
    curvature_ref,
    act,
    grad,
    in_proj,
    out_proj,
    in_feat,
    out_feat,
    total,
    lengths_ref,
    owners_ref,
    starts,
    stops,
    counts,
    act_sems,
    grad_sems,
    first_sems,
):
    tokens = act.shape[0]
    rank = in_proj.shape[0]
    capacity = feature_ref.shape[0]
    queries, slots = placer_ref.shape
    unit = tokens // capacity
    chunks = chunks_of(capacity)

    def copies(index):
        first, size = chunks[index]
        rows = pl.ds(first * unit, size * unit)
        return (
            pltpu.make_async_copy(act_hbm.at[rows], act.at[rows], act_sems.at[index]),
            pltpu.make_async_copy(grad_hbm.at[rows], grad.at[rows], grad_sems.at[index]),
        )

    first_copies = [
        pltpu.make_async_copy(source, target, first_sems.at[place])
        for place, (source, target) in enumerate(
            (
                (in_proj_hbm, in_proj),
                (out_proj_hbm, out_proj),
                (lengths_hbm, lengths_ref),
                (owners_hbm, owners_ref),
            )
        )
    ]
    for copy in first_copies:
        copy.start()
    for index in range(len(chunks)):
        for copy in copies(index):
            copy.start()

    curvature_copy = pltpu.make_async_copy(curvature_hbm, curvature_ref, first_sems.at[4])
    curvature_copy.start()

    for copy in first_copies[2:]:
        copy.wait()
    me = lax.axis_index("row")
    for slot in range(capacity):
        starts[slot] = 0
        stops[slot] = 0
    for owner in range(slots // capacity):
        counts[owner] = 0
    used = jnp.int32(0)
    lane = lax.broadcasted_iota(jnp.int32, (1, slots), 1)
    for example in range(queries):
        owner = owners_ref[example]
        length = lengths_ref[example]
        rank_here = counts[owner]
        counts[owner] = rank_here + 1
        mine = owner == me

        @pl.when(mine)
        def _():
            starts[rank_here] = used
            stops[rank_here] = used + length

        used = used + jnp.where(mine, length, 0)
        placer_ref[pl.ds(example, 1), :] = (
            lane == (owner ^ me) * capacity + rank_here
        ).astype(jnp.float32)
    in_feat[pl.ds(0, unit), :] = jnp.zeros((unit, rank), jnp.float32)
    out_feat[:, pl.ds(0, unit)] = jnp.zeros((rank, unit), jnp.float32)

    for copy in first_copies[:2]:
        copy.wait()
    for index, (first, size) in enumerate(chunks):
        for copy in copies(index):
            copy.wait()
        rows = pl.ds(first * unit, size * unit)
        padded = pl.ds((first + 1) * unit, size * unit)
        in_feat[padded, :] = contract_last(act[rows, :], in_proj[...])
        out_feat[:, padded] = contract_last(grad[rows, :], out_proj[...]).T
    for slot in range(capacity):
        start, stop = starts[slot], stops[slot]
        window = jnp.maximum((stop + unit - 1) // unit - 1, 0) * unit
        window = pl.multiple_of(window, unit)
        position = (
            window - unit + lax.broadcasted_iota(jnp.int32, (rank, 2 * unit), 1)
        )
        member = (position >= start) & (position < stop)
        out_high, out_low = split_two(
            jnp.where(member, out_feat[:, pl.ds(window, 2 * unit)], 0.0)
        )
        in_high, in_low = split_two(in_feat[pl.ds(window, 2 * unit), :])
        total[pl.ds(slot * rank, rank), :] = (
            dot(out_high, in_high) + dot(out_high, in_low) + dot(out_low, in_high)
        )
    for first in range(0, rank, 2):
        pair = [
            total[pl.ds(first + k, capacity, stride=rank), :] for k in range(2)
        ]
        feature_ref[:, pl.ds(first * rank, 2 * rank)] = jnp.concatenate(
            pair, axis=1
        ).astype(jnp.bfloat16)
    curvature_copy.wait()


def featurize(
    activations, out_grads, in_projection, out_projection, curvature, lengths, owners, capacity, slots
):
    tokens, width = activations.shape
    rank = in_projection.shape[0]
    queries = lengths.shape[0]
    unit = tokens // capacity
    chunks = len(chunks_of(capacity))
    return pl.pallas_call(
        featurize_kernel,
        in_specs=[pl.BlockSpec(memory_space=pl.ANY)] * 7,
        out_shape=[
            pltpu.VMEM((capacity, rank * rank), jnp.bfloat16),
            pltpu.VMEM((queries, slots), jnp.float32),
            pltpu.VMEM(curvature.shape, curvature.dtype),
        ],
        out_specs=[pl.BlockSpec(memory_space=pltpu.VMEM)] * 3,
        scratch_shapes=[
            pltpu.VMEM((tokens, width), jnp.bfloat16),
            pltpu.VMEM((tokens, width), jnp.bfloat16),
            pltpu.VMEM((rank, width), jnp.bfloat16),
            pltpu.VMEM((rank, width), jnp.bfloat16),
            pltpu.VMEM((unit + tokens, rank), jnp.float32),
            pltpu.VMEM((rank, unit + tokens), jnp.float32),
            pltpu.VMEM((rank * capacity, rank), jnp.float32),
            pltpu.SMEM((queries,), jnp.int32),
            pltpu.SMEM((queries,), jnp.int32),
            pltpu.SMEM((capacity,), jnp.int32),
            pltpu.SMEM((capacity,), jnp.int32),
            pltpu.SMEM((slots // capacity,), jnp.int32),
            pltpu.SemaphoreType.DMA((chunks,)),
            pltpu.SemaphoreType.DMA((chunks,)),
            pltpu.SemaphoreType.DMA((5,)),
        ],
        compiler_params=pltpu.CompilerParams(vmem_limit_bytes=51 * MIB),
        name="featurize",
    )(lengths, owners, curvature, activations, out_grads, in_projection, out_projection)


def precondition_kernel(curvature_ref, placer_ref, *rest):
    piece_refs, out_ref, feature = rest[:-2], rest[-2], rest[-1]
    capacity = piece_refs[0].shape[0]
    for place, piece_ref in enumerate(piece_refs):
        feature[pl.ds(place * capacity, capacity), :] = piece_ref[...]
    by_slot = contract_last(feature[...], curvature_ref[...]).astype(jnp.bfloat16)
    out_ref[...] = dot(placer_ref[...].astype(jnp.bfloat16), by_slot).astype(jnp.bfloat16)


def precondition(pieces, curvature_rows, placer):
    capacity, entries = pieces[0].shape
    return pl.pallas_call(
        precondition_kernel,
        in_specs=[pl.BlockSpec(memory_space=pltpu.VMEM)] * (2 + len(pieces)),
        out_specs=pl.BlockSpec(memory_space=pltpu.VMEM),
        out_shape=pltpu.VMEM((placer.shape[0], curvature_rows.shape[0]), jnp.bfloat16),
        scratch_shapes=[pltpu.VMEM((len(pieces) * capacity, entries), jnp.bfloat16)],
        compiler_params=pltpu.CompilerParams(vmem_limit_bytes=16 * MIB),
        name="precondition",
    )(curvature_rows, placer, *pieces)


def partial_scores(places, store_ref, piece_refs):
    queries, depth = piece_refs[0].shape
    column = lax.axis_index("row")
    scores = jnp.zeros((store_ref.shape[0], queries), jnp.float32)
    for place, piece_ref in zip(places, piece_refs):
        first = pl.multiple_of((column ^ place) * depth, depth)
        scores += contract_last(store_ref[:, pl.ds(first, depth)], piece_ref[...])
    return scores


def early_score_kernel(places, store_ref, *rest):
    rest[-1][...] = partial_scores(places, store_ref, rest[:-1])


def score_kernel(places, parts, early_ref, store_ref, *rest):
    piece_refs = rest[: -parts - 1]
    share_refs, total = rest[-parts - 1 : -1], rest[-1]
    share = share_refs[0].shape[0]
    total[...] = (early_ref[...] + partial_scores(places, store_ref, piece_refs)).T
    me = lax.axis_index("mod")
    for place in range(parts):
        member = ring_member(lax.rem(ring_place(me) + place, parts))
        row = pl.multiple_of(member * share, share)
        share_refs[place][...] = total[pl.ds(row, share), :]


def score(pieces, store_rows, queries, parts):
    stores = store_rows.shape[0]
    early_places = range(0, len(pieces), 2)
    late_places = range(1, len(pieces), 2)
    early = pl.pallas_call(
        functools.partial(early_score_kernel, early_places),
        in_specs=[pl.BlockSpec(memory_space=pltpu.VMEM)] * (1 + len(early_places)),
        out_specs=pl.BlockSpec(memory_space=pltpu.VMEM),
        out_shape=pltpu.VMEM((stores, queries), jnp.float32),
        compiler_params=pltpu.CompilerParams(vmem_limit_bytes=16 * MIB),
        name="early_score",
    )(store_rows, *[pieces[d] for d in early_places])
    one = pltpu.VMEM((queries // parts, stores), jnp.float32)
    return pl.pallas_call(
        functools.partial(score_kernel, late_places, parts),
        in_specs=[pl.BlockSpec(memory_space=pltpu.VMEM)] * (2 + len(late_places)),
        out_specs=[pl.BlockSpec(memory_space=pltpu.VMEM)] * parts,
        out_shape=[one] * parts,
        scratch_shapes=[pltpu.VMEM((queries, stores), jnp.float32)],
        compiler_params=pltpu.CompilerParams(vmem_limit_bytes=16 * MIB),
        name="score",
    )(early, store_rows, *[pieces[d] for d in late_places])


def exchange(array, axis, distance):
    count = lax.axis_size(axis)
    return lax.ppermute(array, axis, [(i, i ^ distance) for i in range(count)])


def send_on(array, axis, places):
    count = lax.axis_size(axis)
    order = [ring_member(place) for place in range(count)]
    return lax.ppermute(
        array, axis, [(order[i], order[(i + places) % count]) for i in range(count)]
    )


def pieces_of_all(mine, axis):
    count = lax.axis_size(axis)
    far = {0: mine}
    for d in sorted(range(2, count, 2), key=lambda d: -bin(d).count("1")):
        far[d] = exchange(mine, axis, d)
    pieces = []
    for d in range(0, count, 2):
        pieces += [far[d], exchange(far[d], axis, 1)]
    return pieces


def on_device(
    activations,
    out_grads,
    in_projection,
    out_projection,
    inv_curvature,
    store_grads,
    lengths,
    owners,
):
    row_count = lax.axis_size("row")
    mod_count = lax.axis_size("mod")
    queries = lengths.shape[0]
    capacity = 2 * queries // row_count
    feature, placer, curvature = featurize(
        activations[0],
        out_grads[0],
        in_projection[0],
        out_projection[0],
        inv_curvature[0],
        lengths,
        owners,
        capacity,
        row_count * capacity,
    )
    column_part = precondition(pieces_of_all(feature, "row"), curvature, placer)
    shares = score(pieces_of_all(column_part, "row"), store_grads[0], queries, mod_count)
    total = shares[0]
    for places in range(1, mod_count):
        total = total + send_on(shares[places], "mod", places)
    return total


def solution(mesh):
    return jax.shard_map(
        on_device,
        mesh=mesh,
        in_specs=(
            P("mod", "row", None),
            P("mod", "row", None),
            P("mod", None, None),
            P("mod", None, None),
            P("mod", "row", None),
            P("mod", "row", None),
            P(),
            P(),
        ),
        out_specs=P("mod", "row"),
        check_vma=False,
    )
```

```python
import functools

import jax
import jax.numpy as jnp
from jax import lax
from jax.experimental import pallas as pl
from jax.experimental.pallas import tpu as pltpu
from jax.sharding import PartitionSpec as P

MIB = 1024 * 1024


def contract_last(left, right):
    return lax.dot_general(
        left, right, (((1,), (1,)), ((), ())), preferred_element_type=jnp.float32
    )


def ring_member(place):
    return place ^ (place >> 1)


def ring_place(member):
    place = member
    for shift in (1, 2, 4):
        place = place ^ (place >> shift)
    return place


def split_two(values):
    high = values.astype(jnp.bfloat16)
    return high, (values - high.astype(jnp.float32)).astype(jnp.bfloat16)


def dot(left, right):
    return jnp.dot(left, right, preferred_element_type=jnp.float32)


def chunks_of(units):
    return [(first, min(2, units - first)) for first in range(0, units, 2)]


def featurize_kernel(
    lengths_hbm,
    owners_hbm,
    curvature_hbm,
    act_hbm,
    grad_hbm,
    in_proj_hbm,
    out_proj_hbm,
    feature_ref,
    placer_ref,
    curvature_ref,
    act,
    grad,
    in_proj,
    out_proj,
    in_feat,
    out_feat,
    total,
    lengths_ref,
    owners_ref,
    starts,
    stops,
    counts,
    act_sems,
    grad_sems,
    first_sems,
):
    tokens = act.shape[0]
    rank = in_proj.shape[0]
    capacity = feature_ref.shape[0]
    queries, slots = placer_ref.shape
    unit = tokens // capacity
    chunks = chunks_of(capacity)

    def copies(index):
        first, size = chunks[index]
        rows = pl.ds(first * unit, size * unit)
        return (
            pltpu.make_async_copy(act_hbm.at[rows], act.at[rows], act_sems.at[index]),
            pltpu.make_async_copy(grad_hbm.at[rows], grad.at[rows], grad_sems.at[index]),
        )

    first_copies = [
        pltpu.make_async_copy(source, target, first_sems.at[place])
        for place, (source, target) in enumerate(
            (
                (in_proj_hbm, in_proj),
                (out_proj_hbm, out_proj),
                (lengths_hbm, lengths_ref),
                (owners_hbm, owners_ref),
            )
        )
    ]
    for copy in first_copies:
        copy.start()
    for index in range(len(chunks)):
        for copy in copies(index):
            copy.start()

    curvature_copy = pltpu.make_async_copy(curvature_hbm, curvature_ref, first_sems.at[4])
    curvature_copy.start()

    for copy in first_copies[2:]:
        copy.wait()
    me = lax.axis_index("row")
    for slot in range(capacity):
        starts[slot] = 0
        stops[slot] = 0
    for owner in range(slots // capacity):
        counts[owner] = 0
    used = jnp.int32(0)
    lane = lax.broadcasted_iota(jnp.int32, (1, slots), 1)
    for example in range(queries):
        owner = owners_ref[example]
        length = lengths_ref[example]
        rank_here = counts[owner]
        counts[owner] = rank_here + 1
        mine = owner == me

        @pl.when(mine)
        def _():
            starts[rank_here] = used
            stops[rank_here] = used + length

        used = used + jnp.where(mine, length, 0)
        placer_ref[pl.ds(example, 1), :] = (
            lane == (owner ^ me) * capacity + rank_here
        ).astype(jnp.float32)
    in_feat[pl.ds(0, unit), :] = jnp.zeros((unit, rank), jnp.float32)
    out_feat[:, pl.ds(0, unit)] = jnp.zeros((rank, unit), jnp.float32)

    for copy in first_copies[:2]:
        copy.wait()
    for index, (first, size) in enumerate(chunks):
        for copy in copies(index):
            copy.wait()
        rows = pl.ds(first * unit, size * unit)
        padded = pl.ds((first + 1) * unit, size * unit)
        in_feat[padded, :] = contract_last(act[rows, :], in_proj[...])
        out_feat[:, padded] = contract_last(grad[rows, :], out_proj[...]).T
    for slot in range(capacity):
        start, stop = starts[slot], stops[slot]
        window = jnp.maximum((stop + unit - 1) // unit - 1, 0) * unit
        window = pl.multiple_of(window, unit)
        position = (
            window - unit + lax.broadcasted_iota(jnp.int32, (rank, 2 * unit), 1)
        )
        member = (position >= start) & (position < stop)
        out_high, out_low = split_two(
            jnp.where(member, out_feat[:, pl.ds(window, 2 * unit)], 0.0)
        )
        in_high, in_low = split_two(in_feat[pl.ds(window, 2 * unit), :])
        total[pl.ds(slot * rank, rank), :] = (
            dot(out_high, in_high) + dot(out_high, in_low) + dot(out_low, in_high)
        )
    for first in range(0, rank, 2):
        pair = [
            total[pl.ds(first + k, capacity, stride=rank), :] for k in range(2)
        ]
        feature_ref[:, pl.ds(first * rank, 2 * rank)] = jnp.concatenate(
            pair, axis=1
        ).astype(jnp.bfloat16)
    curvature_copy.wait()


def featurize(
    activations, out_grads, in_projection, out_projection, curvature, lengths, owners, capacity, slots
):
    tokens, width = activations.shape
    rank = in_projection.shape[0]
    queries = lengths.shape[0]
    unit = tokens // capacity
    chunks = len(chunks_of(capacity))
    return pl.pallas_call(
        featurize_kernel,
        in_specs=[pl.BlockSpec(memory_space=pl.ANY)] * 7,
        out_shape=[
            pltpu.VMEM((capacity, rank * rank), jnp.bfloat16),
            pltpu.VMEM((queries, slots), jnp.float32),
            pltpu.VMEM(curvature.shape, curvature.dtype),
        ],
        out_specs=[pl.BlockSpec(memory_space=pltpu.VMEM)] * 3,
        scratch_shapes=[
            pltpu.VMEM((tokens, width), jnp.bfloat16),
            pltpu.VMEM((tokens, width), jnp.bfloat16),
            pltpu.VMEM((rank, width), jnp.bfloat16),
            pltpu.VMEM((rank, width), jnp.bfloat16),
            pltpu.VMEM((unit + tokens, rank), jnp.float32),
            pltpu.VMEM((rank, unit + tokens), jnp.float32),
            pltpu.VMEM((rank * capacity, rank), jnp.float32),
            pltpu.SMEM((queries,), jnp.int32),
            pltpu.SMEM((queries,), jnp.int32),
            pltpu.SMEM((capacity,), jnp.int32),
            pltpu.SMEM((capacity,), jnp.int32),
            pltpu.SMEM((slots // capacity,), jnp.int32),
            pltpu.SemaphoreType.DMA((chunks,)),
            pltpu.SemaphoreType.DMA((chunks,)),
            pltpu.SemaphoreType.DMA((5,)),
        ],
        compiler_params=pltpu.CompilerParams(vmem_limit_bytes=51 * MIB),
        name="featurize",
    )(lengths, owners, curvature, activations, out_grads, in_projection, out_projection)


def precondition_kernel(curvature_ref, placer_ref, *rest):
    piece_refs, out_ref, feature = rest[:-2], rest[-2], rest[-1]
    capacity = piece_refs[0].shape[0]
    for place in range(0, len(piece_refs), 2):
        both = [ref[...].astype(jnp.float32) for ref in piece_refs[place : place + 2]]
        feature[pl.ds(place * capacity, 2 * capacity), :] = jnp.concatenate(
            both, axis=0
        ).astype(jnp.bfloat16)
    by_slot = contract_last(feature[...], curvature_ref[...]).astype(jnp.bfloat16)
    out_ref[...] = dot(placer_ref[...].astype(jnp.bfloat16), by_slot).astype(jnp.bfloat16)


def precondition(pieces, curvature_rows, placer):
    capacity, entries = pieces[0].shape
    return pl.pallas_call(
        precondition_kernel,
        in_specs=[pl.BlockSpec(memory_space=pltpu.VMEM)] * (2 + len(pieces)),
        out_specs=pl.BlockSpec(memory_space=pltpu.VMEM),
        out_shape=pltpu.VMEM((placer.shape[0], curvature_rows.shape[0]), jnp.bfloat16),
        scratch_shapes=[pltpu.VMEM((len(pieces) * capacity, entries), jnp.bfloat16)],
        compiler_params=pltpu.CompilerParams(vmem_limit_bytes=16 * MIB),
        name="precondition",
    )(curvature_rows, placer, *pieces)


def partial_scores(places, store_ref, piece_refs):
    queries, depth = piece_refs[0].shape
    column = lax.axis_index("row")
    scores = jnp.zeros((store_ref.shape[0], queries), jnp.float32)
    for place, piece_ref in zip(places, piece_refs):
        first = pl.multiple_of((column ^ place) * depth, depth)
        scores += contract_last(store_ref[:, pl.ds(first, depth)], piece_ref[...])
    return scores


def early_score_kernel(places, store_ref, *rest):
    rest[-1][...] = partial_scores(places, store_ref, rest[:-1])


def score_kernel(places, parts, early_ref, store_ref, *rest):
    piece_refs = rest[: -parts - 1]
    share_refs, total = rest[-parts - 1 : -1], rest[-1]
    share = share_refs[0].shape[0]
    total[...] = (early_ref[...] + partial_scores(places, store_ref, piece_refs)).T
    me = lax.axis_index("mod")
    for place in range(parts):
        member = ring_member(lax.rem(ring_place(me) + place, parts))
        row = pl.multiple_of(member * share, share)
        share_refs[place][...] = total[pl.ds(row, share), :]


def score(pieces, store_rows, queries, parts):
    stores = store_rows.shape[0]
    early_places = range(0, len(pieces), 2)
    late_places = range(1, len(pieces), 2)
    early = pl.pallas_call(
        functools.partial(early_score_kernel, early_places),
        in_specs=[pl.BlockSpec(memory_space=pltpu.VMEM)] * (1 + len(early_places)),
        out_specs=pl.BlockSpec(memory_space=pltpu.VMEM),
        out_shape=pltpu.VMEM((stores, queries), jnp.float32),
        compiler_params=pltpu.CompilerParams(vmem_limit_bytes=16 * MIB),
        name="early_score",
    )(store_rows, *[pieces[d] for d in early_places])
    one = pltpu.VMEM((queries // parts, stores), jnp.float32)
    return pl.pallas_call(
        functools.partial(score_kernel, late_places, parts),
        in_specs=[pl.BlockSpec(memory_space=pltpu.VMEM)] * (2 + len(late_places)),
        out_specs=[pl.BlockSpec(memory_space=pltpu.VMEM)] * parts,
        out_shape=[one] * parts,
        scratch_shapes=[pltpu.VMEM((queries, stores), jnp.float32)],
        compiler_params=pltpu.CompilerParams(vmem_limit_bytes=16 * MIB),
        name="score",
    )(early, store_rows, *[pieces[d] for d in late_places])


def exchange(array, axis, distance):
    count = lax.axis_size(axis)
    return lax.ppermute(array, axis, [(i, i ^ distance) for i in range(count)])


def send_on(array, axis, places):
    count = lax.axis_size(axis)
    order = [ring_member(place) for place in range(count)]
    return lax.ppermute(
        array, axis, [(order[i], order[(i + places) % count]) for i in range(count)]
    )


def pieces_of_all(mine, axis):
    count = lax.axis_size(axis)
    far = {0: mine}
    for d in sorted(range(2, count, 2), key=lambda d: -bin(d).count("1")):
        far[d] = exchange(mine, axis, d)
    pieces = []
    for d in range(0, count, 2):
        pieces += [far[d], exchange(far[d], axis, 1)]
    return pieces


def on_device(
    activations,
    out_grads,
    in_projection,
    out_projection,
    inv_curvature,
    store_grads,
    lengths,
    owners,
):
    row_count = lax.axis_size("row")
    mod_count = lax.axis_size("mod")
    queries = lengths.shape[0]
    capacity = 2 * queries // row_count
    feature, placer, curvature = featurize(
        activations[0],
        out_grads[0],
        in_projection[0],
        out_projection[0],
        inv_curvature[0],
        lengths,
        owners,
        capacity,
        row_count * capacity,
    )
    column_part = precondition(pieces_of_all(feature, "row"), curvature, placer)
    shares = score(pieces_of_all(column_part, "row"), store_grads[0], queries, mod_count)
    total = shares[0]
    for places in range(1, mod_count):
        total = total + send_on(shares[places], "mod", places)
    return total


def solution(mesh):
    return jax.shard_map(
        on_device,
        mesh=mesh,
        in_specs=(
            P("mod", "row", None),
            P("mod", "row", None),
            P("mod", None, None),
            P("mod", None, None),
            P("mod", "row", None),
            P("mod", "row", None),
            P(),
            P(),
        ),
        out_specs=P("mod", "row"),
        check_vma=False,
    )
```

```python
import functools

import jax
import jax.numpy as jnp
from jax import lax
from jax.experimental import pallas as pl
from jax.experimental.pallas import tpu as pltpu
from jax.sharding import PartitionSpec as P

MIB = 1024 * 1024


def contract_last(left, right):
    return lax.dot_general(
        left, right, (((1,), (1,)), ((), ())), preferred_element_type=jnp.float32
    )


def ring_member(place):
    return place ^ (place >> 1)


def ring_place(member):
    place = member
    for shift in (1, 2, 4):
        place = place ^ (place >> shift)
    return place


def split_two(values):
    high = values.astype(jnp.bfloat16)
    return high, (values - high.astype(jnp.float32)).astype(jnp.bfloat16)


def dot(left, right):
    return jnp.dot(left, right, preferred_element_type=jnp.float32)


def featurize_kernel(
    lengths_hbm,
    owners_hbm,
    curvature_hbm,
    act_hbm,
    grad_hbm,
    in_proj_hbm,
    out_proj_hbm,
    feature_ref,
    placer_ref,
    curvature_ref,
    act,
    grad,
    in_proj,
    out_proj,
    in_feat,
    out_feat,
    total,
    lengths_ref,
    owners_ref,
    starts,
    stops,
    counts,
    act_sems,
    grad_sems,
    first_sems,
):
    tokens = act.shape[0]
    rank = in_proj.shape[0]
    capacity = feature_ref.shape[0]
    queries, slots = placer_ref.shape
    unit = tokens // capacity
    chunks = act_sems.shape[0]
    size = tokens // chunks

    def copies(index):
        rows = pl.ds(pl.multiple_of(index * size, size), size)
        return (
            pltpu.make_async_copy(act_hbm.at[rows], act.at[rows], act_sems.at[index]),
            pltpu.make_async_copy(grad_hbm.at[rows], grad.at[rows], grad_sems.at[index]),
        )

    first_copies = [
        pltpu.make_async_copy(source, target, first_sems.at[place])
        for place, (source, target) in enumerate(
            (
                (in_proj_hbm, in_proj),
                (out_proj_hbm, out_proj),
                (lengths_hbm, lengths_ref),
                (owners_hbm, owners_ref),
            )
        )
    ]
    for copy in first_copies:
        copy.start()
    for index in range(chunks):
        for copy in copies(index):
            copy.start()

    curvature_copy = pltpu.make_async_copy(curvature_hbm, curvature_ref, first_sems.at[4])
    curvature_copy.start()

    for copy in first_copies[2:]:
        copy.wait()
    me = lax.axis_index("row")
    for slot in range(capacity):
        starts[slot] = 0
        stops[slot] = 0
    for owner in range(slots // capacity):
        counts[owner] = 0
    used = jnp.int32(0)
    lane = lax.broadcasted_iota(jnp.int32, (1, slots), 1)
    for example in range(queries):
        owner = owners_ref[example]
        length = lengths_ref[example]
        rank_here = counts[owner]
        counts[owner] = rank_here + 1
        mine = owner == me

        @pl.when(mine)
        def _():
            starts[rank_here] = used
            stops[rank_here] = used + length

        used = used + jnp.where(mine, length, 0)
        placer_ref[pl.ds(example, 1), :] = (
            lane == (owner ^ me) * capacity + rank_here
        ).astype(jnp.float32)
    in_feat[pl.ds(0, unit), :] = jnp.zeros((unit, rank), jnp.float32)
    out_feat[:, pl.ds(0, unit)] = jnp.zeros((rank, unit), jnp.float32)

    for copy in first_copies[:2]:
        copy.wait()
    @pl.loop(0, chunks)
    def _(index):
        for copy in copies(index):
            copy.wait()
        rows = pl.ds(pl.multiple_of(index * size, size), size)
        padded = pl.ds(pl.multiple_of(index * size + unit, unit), size)
        in_feat[padded, :] = contract_last(act[rows, :], in_proj[...])
        out_feat[:, padded] = contract_last(grad[rows, :], out_proj[...]).T

    @pl.loop(0, capacity, unroll=capacity)
    def _(slot):
        start, stop = starts[slot], stops[slot]
        window = jnp.maximum((stop + unit - 1) // unit - 1, 0) * unit
        window = pl.multiple_of(window, unit)
        position = window - unit + lax.broadcasted_iota(jnp.int32, (rank, 2 * unit), 1)
        member = (position >= start) & (position < stop)
        out_high, out_low = split_two(
            jnp.where(member, out_feat[:, pl.ds(window, 2 * unit)], 0.0)
        )
        in_high, in_low = split_two(in_feat[pl.ds(window, 2 * unit), :])
        total[pl.ds(pl.multiple_of(slot * rank, rank), rank), :] = (
            dot(out_high, in_high) + dot(out_high, in_low) + dot(out_low, in_high)
        )

    for first in range(0, rank, 2):
        pair = [
            total[pl.ds(first + k, capacity, stride=rank), :] for k in range(2)
        ]
        feature_ref[:, pl.ds(first * rank, 2 * rank)] = jnp.concatenate(
            pair, axis=1
        ).astype(jnp.bfloat16)
    curvature_copy.wait()


def featurize(
    activations, out_grads, in_projection, out_projection, curvature, lengths, owners, capacity, slots
):
    tokens, width = activations.shape
    rank = in_projection.shape[0]
    queries = lengths.shape[0]
    unit = tokens // capacity
    chunks = max(capacity // 2, 1)
    return pl.pallas_call(
        featurize_kernel,
        in_specs=[pl.BlockSpec(memory_space=pl.ANY)] * 7,
        out_shape=[
            pltpu.VMEM((capacity, rank * rank), jnp.bfloat16),
            pltpu.VMEM((queries, slots), jnp.float32),
            pltpu.VMEM(curvature.shape, curvature.dtype),
        ],
        out_specs=[pl.BlockSpec(memory_space=pltpu.VMEM)] * 3,
        scratch_shapes=[
            pltpu.VMEM((tokens, width), jnp.bfloat16),
            pltpu.VMEM((tokens, width), jnp.bfloat16),
            pltpu.VMEM((rank, width), jnp.bfloat16),
            pltpu.VMEM((rank, width), jnp.bfloat16),
            pltpu.VMEM((unit + tokens, rank), jnp.float32),
            pltpu.VMEM((rank, unit + tokens), jnp.float32),
            pltpu.VMEM((rank * capacity, rank), jnp.float32),
            pltpu.SMEM((queries,), jnp.int32),
            pltpu.SMEM((queries,), jnp.int32),
            pltpu.SMEM((capacity,), jnp.int32),
            pltpu.SMEM((capacity,), jnp.int32),
            pltpu.SMEM((slots // capacity,), jnp.int32),
            pltpu.SemaphoreType.DMA((chunks,)),
            pltpu.SemaphoreType.DMA((chunks,)),
            pltpu.SemaphoreType.DMA((5,)),
        ],
        compiler_params=pltpu.CompilerParams(vmem_limit_bytes=51 * MIB),
        name="featurize",
    )(lengths, owners, curvature, activations, out_grads, in_projection, out_projection)


def precondition_kernel(curvature_ref, placer_ref, *rest):
    piece_refs, out_ref, feature = rest[:-2], rest[-2], rest[-1]
    capacity = piece_refs[0].shape[0]
    for place in range(0, len(piece_refs), 2):
        both = [ref[...].astype(jnp.float32) for ref in piece_refs[place : place + 2]]
        feature[pl.ds(place * capacity, 2 * capacity), :] = jnp.concatenate(
            both, axis=0
        ).astype(jnp.bfloat16)
    by_slot = contract_last(curvature_ref[...], feature[...]).T.astype(jnp.bfloat16)
    out_ref[...] = dot(placer_ref[...].astype(jnp.bfloat16), by_slot).astype(jnp.bfloat16)


def precondition(pieces, curvature_rows, placer):
    capacity, entries = pieces[0].shape
    return pl.pallas_call(
        precondition_kernel,
        in_specs=[pl.BlockSpec(memory_space=pltpu.VMEM)] * (2 + len(pieces)),
        out_specs=pl.BlockSpec(memory_space=pltpu.VMEM),
        out_shape=pltpu.VMEM((placer.shape[0], curvature_rows.shape[0]), jnp.bfloat16),
        scratch_shapes=[pltpu.VMEM((len(pieces) * capacity, entries), jnp.bfloat16)],
        compiler_params=pltpu.CompilerParams(vmem_limit_bytes=16 * MIB),
        name="precondition",
    )(curvature_rows, placer, *pieces)


def partial_scores(places, store_ref, piece_refs):
    queries, depth = piece_refs[0].shape
    column = lax.axis_index("row")
    scores = jnp.zeros((store_ref.shape[0], queries), jnp.float32)
    for place, piece_ref in zip(places, piece_refs):
        first = pl.multiple_of((column ^ place) * depth, depth)
        scores += contract_last(store_ref[:, pl.ds(first, depth)], piece_ref[...])
    return scores


def early_score_kernel(places, store_ref, *rest):
    rest[-1][...] = partial_scores(places, store_ref, rest[:-1])


def score_kernel(places, parts, early_ref, store_ref, *rest):
    piece_refs = rest[: -parts - 1]
    share_refs, total = rest[-parts - 1 : -1], rest[-1]
    share = share_refs[0].shape[0]
    total[...] = (early_ref[...] + partial_scores(places, store_ref, piece_refs)).T
    me = lax.axis_index("mod")
    for place in range(parts):
        member = ring_member(lax.rem(ring_place(me) + place, parts))
        row = pl.multiple_of(member * share, share)
        share_refs[place][...] = total[pl.ds(row, share), :]


def score(pieces, store_rows, queries, parts):
    stores = store_rows.shape[0]
    early_places = range(0, len(pieces), 2)
    late_places = range(1, len(pieces), 2)
    early = pl.pallas_call(
        functools.partial(early_score_kernel, early_places),
        in_specs=[pl.BlockSpec(memory_space=pltpu.VMEM)] * (1 + len(early_places)),
        out_specs=pl.BlockSpec(memory_space=pltpu.VMEM),
        out_shape=pltpu.VMEM((stores, queries), jnp.float32),
        compiler_params=pltpu.CompilerParams(vmem_limit_bytes=16 * MIB),
        name="early_score",
    )(store_rows, *[pieces[d] for d in early_places])
    one = pltpu.VMEM((queries // parts, stores), jnp.float32)
    return pl.pallas_call(
        functools.partial(score_kernel, late_places, parts),
        in_specs=[pl.BlockSpec(memory_space=pltpu.VMEM)] * (2 + len(late_places)),
        out_specs=[pl.BlockSpec(memory_space=pltpu.VMEM)] * parts,
        out_shape=[one] * parts,
        scratch_shapes=[pltpu.VMEM((queries, stores), jnp.float32)],
        compiler_params=pltpu.CompilerParams(vmem_limit_bytes=16 * MIB),
        name="score",
    )(early, store_rows, *[pieces[d] for d in late_places])


def exchange(array, axis, distance):
    count = lax.axis_size(axis)
    return lax.ppermute(array, axis, [(i, i ^ distance) for i in range(count)])


def send_on(array, axis, places):
    count = lax.axis_size(axis)
    order = [ring_member(place) for place in range(count)]
    return lax.ppermute(
        array, axis, [(order[i], order[(i + places) % count]) for i in range(count)]
    )


def pieces_of_all(mine, axis):
    count = lax.axis_size(axis)
    far = {0: mine}
    for d in sorted(range(2, count, 2), key=lambda d: -bin(d).count("1")):
        far[d] = exchange(mine, axis, d)
    pieces = []
    for d in range(0, count, 2):
        pieces += [far[d], exchange(far[d], axis, 1)]
    return pieces


def on_device(
    activations,
    out_grads,
    in_projection,
    out_projection,
    inv_curvature,
    store_grads,
    lengths,
    owners,
):
    row_count = lax.axis_size("row")
    mod_count = lax.axis_size("mod")
    queries = lengths.shape[0]
    capacity = 2 * queries // row_count
    feature, placer, curvature = featurize(
        activations[0],
        out_grads[0],
        in_projection[0],
        out_projection[0],
        inv_curvature[0],
        lengths,
        owners,
        capacity,
        row_count * capacity,
    )
    column_part = precondition(pieces_of_all(feature, "row"), curvature, placer)
    shares = score(pieces_of_all(column_part, "row"), store_grads[0], queries, mod_count)
    total = shares[0]
    for places in range(1, mod_count):
        total = total + send_on(shares[places], "mod", places)
    return total


def solution(mesh):
    return jax.shard_map(
        on_device,
        mesh=mesh,
        in_specs=(
            P("mod", "row", None),
            P("mod", "row", None),
            P("mod", None, None),
            P("mod", None, None),
            P("mod", "row", None),
            P("mod", "row", None),
            P(),
            P(),
        ),
        out_specs=P("mod", "row"),
        check_vma=False,
    )
```

```python
import functools

import jax
import jax.numpy as jnp
from jax import lax
from jax.experimental import pallas as pl
from jax.experimental.pallas import tpu as pltpu
from jax.sharding import PartitionSpec as P

MIB = 1024 * 1024


def contract_last(left, right):
    return lax.dot_general(
        left, right, (((1,), (1,)), ((), ())), preferred_element_type=jnp.float32
    )


def ring_member(place):
    return place ^ (place >> 1)


def ring_place(member):
    place = member
    for shift in (1, 2, 4):
        place = place ^ (place >> shift)
    return place


def split_two(values):
    high = values.astype(jnp.bfloat16)
    return high, (values - high.astype(jnp.float32)).astype(jnp.bfloat16)


def dot(left, right):
    return jnp.dot(left, right, preferred_element_type=jnp.float32)


def featurize_kernel(
    lengths_hbm,
    owners_hbm,
    curvature_hbm,
    act_hbm,
    grad_hbm,
    in_proj_hbm,
    out_proj_hbm,
    feature_ref,
    placer_ref,
    curvature_ref,
    act,
    grad,
    in_proj,
    out_proj,
    in_feat,
    out_feat,
    total,
    lengths_ref,
    owners_ref,
    starts,
    stops,
    counts,
    act_sems,
    grad_sems,
    first_sems,
):
    tokens = act.shape[0]
    rank = in_proj.shape[0]
    capacity = feature_ref.shape[0]
    queries, slots = placer_ref.shape
    unit = tokens // capacity
    chunks = act_sems.shape[0]
    size = tokens // chunks

    def copies(index):
        rows = pl.ds(pl.multiple_of(index * size, size), size)
        return (
            pltpu.make_async_copy(act_hbm.at[rows], act.at[rows], act_sems.at[index]),
            pltpu.make_async_copy(grad_hbm.at[rows], grad.at[rows], grad_sems.at[index]),
        )

    first_copies = [
        pltpu.make_async_copy(source, target, first_sems.at[place])
        for place, (source, target) in enumerate(
            (
                (in_proj_hbm, in_proj),
                (out_proj_hbm, out_proj),
                (lengths_hbm, lengths_ref),
                (owners_hbm, owners_ref),
            )
        )
    ]
    for copy in first_copies:
        copy.start()
    for index in range(chunks):
        for copy in copies(index):
            copy.start()

    curvature_copy = pltpu.make_async_copy(curvature_hbm, curvature_ref, first_sems.at[4])
    curvature_copy.start()

    for copy in first_copies[2:]:
        copy.wait()
    me = lax.axis_index("row")
    for slot in range(capacity):
        starts[slot] = 0
        stops[slot] = 0
    for owner in range(slots // capacity):
        counts[owner] = 0
    used = jnp.int32(0)
    lane = lax.broadcasted_iota(jnp.int32, (1, slots), 1)
    for example in range(queries):
        owner = owners_ref[example]
        length = lengths_ref[example]
        rank_here = counts[owner]
        counts[owner] = rank_here + 1
        mine = owner == me

        @pl.when(mine)
        def _():
            starts[rank_here] = used
            stops[rank_here] = used + length

        used = used + jnp.where(mine, length, 0)
        placer_ref[pl.ds(example, 1), :] = (
            lane == (owner ^ me) * capacity + rank_here
        ).astype(jnp.float32)
    in_feat[pl.ds(0, unit), :] = jnp.zeros((unit, rank), jnp.float32)
    out_feat[:, pl.ds(0, unit)] = jnp.zeros((rank, unit), jnp.float32)

    for copy in first_copies[:2]:
        copy.wait()
    @pl.loop(0, chunks)
    def _(index):
        for copy in copies(index):
            copy.wait()
        rows = pl.ds(pl.multiple_of(index * size, size), size)
        padded = pl.ds(pl.multiple_of(index * size + unit, unit), size)
        in_feat[padded, :] = contract_last(act[rows, :], in_proj[...])
        out_feat[:, padded] = contract_last(grad[rows, :], out_proj[...]).T

    @pl.loop(0, capacity, unroll=capacity)
    def _(slot):
        start, stop = starts[slot], stops[slot]
        window = jnp.maximum((stop + unit - 1) // unit - 1, 0) * unit
        window = pl.multiple_of(window, unit)
        position = window - unit + lax.broadcasted_iota(jnp.int32, (rank, 2 * unit), 1)
        member = (position >= start) & (position < stop)
        out_high, out_low = split_two(
            jnp.where(member, out_feat[:, pl.ds(window, 2 * unit)], 0.0)
        )
        in_high, in_low = split_two(in_feat[pl.ds(window, 2 * unit), :])
        total[pl.ds(pl.multiple_of(slot * rank, rank), rank), :] = (
            dot(out_high, in_high) + dot(out_high, in_low) + dot(out_low, in_high)
        )

    for first in range(0, rank, 2):
        pair = [
            total[pl.ds(first + k, capacity, stride=rank), :] for k in range(2)
        ]
        feature_ref[:, pl.ds(first * rank, 2 * rank)] = jnp.concatenate(
            pair, axis=1
        ).astype(jnp.bfloat16)
    curvature_copy.wait()


def featurize(
    activations, out_grads, in_projection, out_projection, curvature, lengths, owners, capacity, slots
):
    tokens, width = activations.shape
    rank = in_projection.shape[0]
    queries = lengths.shape[0]
    unit = tokens // capacity
    chunks = max(capacity // 2, 1)
    return pl.pallas_call(
        featurize_kernel,
        in_specs=[pl.BlockSpec(memory_space=pl.ANY)] * 7,
        out_shape=[
            pltpu.VMEM((capacity, rank * rank), jnp.bfloat16),
            pltpu.VMEM((queries, slots), jnp.float32),
            pltpu.VMEM(curvature.shape, curvature.dtype),
        ],
        out_specs=[pl.BlockSpec(memory_space=pltpu.VMEM)] * 3,
        scratch_shapes=[
            pltpu.VMEM((tokens, width), jnp.bfloat16),
            pltpu.VMEM((tokens, width), jnp.bfloat16),
            pltpu.VMEM((rank, width), jnp.bfloat16),
            pltpu.VMEM((rank, width), jnp.bfloat16),
            pltpu.VMEM((unit + tokens, rank), jnp.float32),
            pltpu.VMEM((rank, unit + tokens), jnp.float32),
            pltpu.VMEM((rank * capacity, rank), jnp.float32),
            pltpu.SMEM((queries,), jnp.int32),
            pltpu.SMEM((queries,), jnp.int32),
            pltpu.SMEM((capacity,), jnp.int32),
            pltpu.SMEM((capacity,), jnp.int32),
            pltpu.SMEM((slots // capacity,), jnp.int32),
            pltpu.SemaphoreType.DMA((chunks,)),
            pltpu.SemaphoreType.DMA((chunks,)),
            pltpu.SemaphoreType.DMA((5,)),
        ],
        compiler_params=pltpu.CompilerParams(vmem_limit_bytes=51 * MIB),
        name="featurize",
    )(lengths, owners, curvature, activations, out_grads, in_projection, out_projection)


def precondition_kernel(curvature_ref, placer_ref, *rest):
    piece_refs, out_ref, feature = rest[:-2], rest[-2], rest[-1]
    capacity = piece_refs[0].shape[0]
    for place in range(0, len(piece_refs), 2):
        both = [ref[...].astype(jnp.float32) for ref in piece_refs[place : place + 2]]
        feature[pl.ds(place * capacity, 2 * capacity), :] = jnp.concatenate(
            both, axis=0
        ).astype(jnp.bfloat16)
    by_slot = contract_last(curvature_ref[...], feature[...]).T.astype(jnp.bfloat16)
    out_ref[...] = dot(placer_ref[...].astype(jnp.bfloat16), by_slot).astype(jnp.bfloat16)


def precondition(pieces, curvature_rows, placer):
    capacity, entries = pieces[0].shape
    return pl.pallas_call(
        precondition_kernel,
        in_specs=[pl.BlockSpec(memory_space=pltpu.VMEM)] * (2 + len(pieces)),
        out_specs=pl.BlockSpec(memory_space=pltpu.VMEM),
        out_shape=pltpu.VMEM((placer.shape[0], curvature_rows.shape[0]), jnp.bfloat16),
        scratch_shapes=[pltpu.VMEM((len(pieces) * capacity, entries), jnp.bfloat16)],
        compiler_params=pltpu.CompilerParams(vmem_limit_bytes=16 * MIB),
        name="precondition",
    )(curvature_rows, placer, *pieces)


def partial_scores(places, store_ref, piece_refs):
    queries, depth = piece_refs[0].shape
    column = lax.axis_index("row")
    scores = jnp.zeros((store_ref.shape[0], queries), jnp.float32)
    for place, piece_ref in zip(places, piece_refs):
        first = pl.multiple_of((column ^ place) * depth, depth)
        scores += contract_last(store_ref[:, pl.ds(first, depth)], piece_ref[...])
    return scores


def early_score_kernel(places, store_ref, *rest):
    rest[-1][...] = partial_scores(places, store_ref, rest[:-1])


def score_kernel(places, parts, early_ref, store_ref, *rest):
    piece_refs = rest[: -parts - 1]
    share_refs, total = rest[-parts - 1 : -1], rest[-1]
    share = share_refs[0].shape[0]
    total[...] = (early_ref[...] + partial_scores(places, store_ref, piece_refs)).T
    me = lax.axis_index("mod")
    for place in range(parts):
        member = ring_member(lax.rem(ring_place(me) + place, parts))
        row = pl.multiple_of(member * share, share)
        share_refs[place][...] = total[pl.ds(row, share), :]


def score(pieces, store_rows, queries, parts):
    stores = store_rows.shape[0]
    early_places = range(0, len(pieces), 2)
    late_places = range(1, len(pieces), 2)
    early = pl.pallas_call(
        functools.partial(early_score_kernel, early_places),
        in_specs=[pl.BlockSpec(memory_space=pltpu.VMEM)] * (1 + len(early_places)),
        out_specs=pl.BlockSpec(memory_space=pltpu.VMEM),
        out_shape=pltpu.VMEM((stores, queries), jnp.float32),
        compiler_params=pltpu.CompilerParams(vmem_limit_bytes=16 * MIB),
        name="early_score",
    )(store_rows, *[pieces[d] for d in early_places])
    one = pltpu.VMEM((queries // parts, stores), jnp.float32)
    return pl.pallas_call(
        functools.partial(score_kernel, late_places, parts),
        in_specs=[pl.BlockSpec(memory_space=pltpu.VMEM)] * (2 + len(late_places)),
        out_specs=[pl.BlockSpec(memory_space=pltpu.VMEM)] * parts,
        out_shape=[one] * parts,
        scratch_shapes=[pltpu.VMEM((queries, stores), jnp.float32)],
        compiler_params=pltpu.CompilerParams(vmem_limit_bytes=16 * MIB),
        name="score",
    )(early, store_rows, *[pieces[d] for d in late_places])


def exchange(array, axis, distance):
    count = lax.axis_size(axis)
    return lax.ppermute(array, axis, [(i, i ^ distance) for i in range(count)])


def send_on(array, axis, places):
    count = lax.axis_size(axis)
    order = [ring_member(place) for place in range(count)]
    return lax.ppermute(
        array, axis, [(order[i], order[(i + places) % count]) for i in range(count)]
    )


def pieces_of_all(mine, axis):
    count = lax.axis_size(axis)
    far = {0: mine}
    for d in sorted(range(2, count, 2), key=lambda d: -bin(d).count("1")):
        far[d] = exchange(mine, axis, d)
    pieces = []
    for d in range(0, count, 2):
        pieces += [far[d], exchange(far[d], axis, 1)]
    return pieces


def add_up_kernel(*refs):
    refs[-1][...] = sum(ref[...] for ref in refs[1:-1]) + refs[0][...]


def add_up(arrays):
    return pl.pallas_call(
        add_up_kernel,
        in_specs=[pl.BlockSpec(memory_space=pltpu.VMEM)] * len(arrays),
        out_specs=pl.BlockSpec(memory_space=pltpu.VMEM),
        out_shape=jax.ShapeDtypeStruct(arrays[0].shape, arrays[0].dtype),
        name="add_up",
    )(*arrays)


def on_device(
    activations,
    out_grads,
    in_projection,
    out_projection,
    inv_curvature,
    store_grads,
    lengths,
    owners,
):
    row_count = lax.axis_size("row")
    mod_count = lax.axis_size("mod")
    queries = lengths.shape[0]
    capacity = 2 * queries // row_count
    feature, placer, curvature = featurize(
        activations[0],
        out_grads[0],
        in_projection[0],
        out_projection[0],
        inv_curvature[0],
        lengths,
        owners,
        capacity,
        row_count * capacity,
    )
    column_part = precondition(pieces_of_all(feature, "row"), curvature, placer)
    shares = score(pieces_of_all(column_part, "row"), store_grads[0], queries, mod_count)
    arrived = [send_on(shares[places], "mod", places) for places in range(1, mod_count)]
    return add_up([shares[0], *arrived])


def solution(mesh):
    return jax.shard_map(
        on_device,
        mesh=mesh,
        in_specs=(
            P("mod", "row", None),
            P("mod", "row", None),
            P("mod", None, None),
            P("mod", None, None),
            P("mod", "row", None),
            P("mod", "row", None),
            P(),
            P(),
        ),
        out_specs=P("mod", "row"),
        check_vma=False,
    )
```
